512 devices in a mesh: ctx: 32 (over z, core), tp: 16 (over x, y).
Axes of the slice: x: 4, y: 4, z: 16, core: 2. Of those that a mesh axis runs over, the one named last changes fastest.
Arguments:
- inputs: bfloat16 [4096, 4096], P('ctx'), may hold values from -6 to 6
- w_in: bfloat16 [4096, 4096], P('ctx', 'tp'), may hold values from -0.09375 to 0.09375
- b_in: bfloat16 [4096, 128], P('ctx'), may hold values from -0.25 to 0.25
- c_in: bfloat16 [4096, 128], P('ctx'), may hold values from -0.75 to 0.75
- log_decay: float32 [4096, 64], P('ctx', 'tp'), may hold values from -0.75 to 0, as said below
- skip: float32 [64], P('tp'), may hold values from 0.5 to 1.5
- d_out: bfloat16 [4096, 4096], P('ctx', 'tp'), may hold values from -0.0234375 to 0.0234375
Outputs:
- d_w: float32 [4096, 4096], P('ctx', 'tp')
- d_b: float32 [4096, 128], P('ctx')
- d_c: float32 [4096, 128], P('ctx')
The draws below stay inside these ranges and needn't reach their ends.
Inputs may be any that keep to these rules, and one draw needn't show every extreme that they name: `log_decay`: never positive.
All inputs are finite; a program needn't handle non-finite values.
Results may differ from the reference program's by a relative error of at most 0.0034.
Values may be sent and summed in bfloat16 or wider, within the bound.
A program may use at most 64 MiB of HBM per device.

```python
import math
import jax
import jax.numpy as jnp
from jax import lax

WIDTH = 4096
ATTENTION_UNITS = 64
HEAD_DIM = 64
STATE = 128
TOK_DEV = 128
SEQUENCE_LENGTH = 4096
INNER = 4096


def draw_log_decay(key, part):
    key = jax.random.fold_in(key, 7)
    sampler_seeds = jax.random.split(key, 5)
    fast_share = 0.5
    quick_decay_heads = jax.random.uniform(sampler_seeds[0], (ATTENTION_UNITS,)) < fast_share
    base_rate = jnp.where(quick_decay_heads, 1.0 / 40.0, 0.25 / SEQUENCE_LENGTH)
    shard_count = SEQUENCE_LENGTH // TOK_DEV
    shard_factor = jnp.exp(jax.random.uniform(sampler_seeds[1], (shard_count, ATTENTION_UNITS), jnp.float32, math.log(0.5), math.log(2.0)))
    shard_factor = jnp.repeat(shard_factor, TOK_DEV, axis=0)
    jitter = jnp.exp(jax.random.uniform(sampler_seeds[2], (SEQUENCE_LENGTH, ATTENTION_UNITS), jnp.float32, math.log(0.7), math.log(1.4)))
    shard_partitions = jax.random.uniform(sampler_seeds[3], (SEQUENCE_LENGTH, ATTENTION_UNITS)) < 2.0 / SEQUENCE_LENGTH
    objective_scalars = jax.random.uniform(sampler_seeds[4], (SEQUENCE_LENGTH, ATTENTION_UNITS), jnp.float32, math.log(0.6), math.log(0.8))
    forgetting_factors = -base_rate[None, :] * shard_factor * jitter
    return (forgetting_factors + jnp.where(shard_partitions, objective_scalars, 0.0)).astype(jnp.float32)


def shard_levels(key, extent, cuts, low, top_value):
    def one(axis_at, blocks):
        steps = jax.random.uniform(jax.random.fold_in(jax.random.fold_in(key, 6), axis_at), (blocks,), jnp.float32, low / len(cuts), top_value / len(cuts))
        return jnp.repeat(jnp.exp(steps), extent[axis_at] // blocks).reshape((-1,) + (1,) * (len(extent) - axis_at - 1))

    loudness = one(*cuts[0])
    for cut in cuts[1:]:
        loudness = loudness * one(*cut)
    return loudness


def normal_values(rng, extent, scale, bound, shards=(), dtype=jnp.bfloat16):
    values = jax.random.normal(rng, extent, jnp.float32) * scale
    if len(shards) > 0:
        values = shard_levels(rng, extent, shards, -0.22, 0.18) * values
    return jnp.clip(values, min=-bound, max=bound).astype(dtype)


def setup_inputs(seed: int = 0) -> dict:
    splits = jax.random.split(jax.random.key(seed), 8)
    inputs = normal_values(splits[0], (SEQUENCE_LENGTH, WIDTH), 1.0, 6.0, ((0, 32),))
    w_in = normal_values(splits[1], (WIDTH, INNER), WIDTH ** -0.5, 0.09375, ((0, 32), (1, 16)))
    b_in = normal_values(splits[2], (SEQUENCE_LENGTH, STATE), (4 * STATE) ** -0.5, 0.25, ((0, 32),))
    c_in = normal_values(splits[3], (SEQUENCE_LENGTH, STATE), (max(SEQUENCE_LENGTH // 64, 1)) ** -0.5, 0.75, ((0, 32),))
    log_decay = draw_log_decay(jax.random.fold_in(splits[7], 71), 0)
    skip = jnp.clip(0.5 + 1.0 * jax.random.uniform(splits[5], (ATTENTION_UNITS,), jnp.float32) ** shard_levels(splits[5], (ATTENTION_UNITS,), ((0, 16),), -0.2, 0.2), 0.5, 1.5)
    d_out = normal_values(splits[6], (SEQUENCE_LENGTH, INNER), (16 * SEQUENCE_LENGTH) ** -0.5, 0.0234375, ((0, 32), (1, 16)))
    return dict(inputs=inputs, w_in=w_in, b_in=b_in, c_in=c_in, log_decay=log_decay, skip=skip, d_out=d_out)


def block_ends(packed):
    values_b, upstream_b, b_block, c_block, decay_b = packed
    cumulative = jnp.cumsum(decay_b, axis=0)
    block_log = cumulative[TOK_DEV - 1]
    to_end = jnp.exp(block_log[None, :] - cumulative)
    from_start = jnp.exp(cumulative)
    state_end = jnp.einsum("lh,ln,lhp->hnp", to_end, b_block.astype(jnp.float32), values_b.astype(jnp.float32), precision=lax.Precision.HIGHEST)
    adjoint_start = jnp.einsum("lh,ln,lhp->hnp", from_start, c_block.astype(jnp.float32), upstream_b.astype(jnp.float32), precision=lax.Precision.HIGHEST)
    return jnp.exp(block_log), state_end, adjoint_start


def block_grads_skip(packed, skip):
    values_b, upstream_b, b_block, c_block, decay_b, state_in, adjoint_in = packed
    cumulative = jnp.cumsum(decay_b, axis=0)
    block_log = cumulative[TOK_DEV - 1]
    to_end = jnp.exp(block_log[None, :] - cumulative)
    from_start = jnp.exp(cumulative)
    positions = jnp.arange(TOK_DEV)
    causal = (positions[:, None] >= positions[None, :])[None]
    decay_rows = cumulative.T
    log_gap = decay_rows[:, :, None] - decay_rows[:, None, :]
    within = jnp.where(causal, jnp.exp(jnp.where(causal, log_gap, 0.0)), 0.0)
    scores = jnp.einsum("sn,tn->st", c_block, b_block, preferred_element_type=jnp.float32)
    mixing = (within * scores[None]).astype(jnp.bfloat16)
    b_float = b_block.astype(jnp.float32)
    values_float = values_b.astype(jnp.float32)
    upstream_float = upstream_b.astype(jnp.float32)
    grad_local = jnp.einsum("hst,shp->thp", mixing, upstream_b, preferred_element_type=jnp.float32)
    grad_carried = to_end[:, :, None] * jnp.einsum("tn,hnp->thp", b_float, adjoint_in, precision=lax.Precision.HIGHEST)
    grad_values = (grad_local + grad_carried + skip[None, :, None] * upstream_float).astype(jnp.bfloat16)
    gram = jnp.einsum("thp,shp->hts", upstream_b, values_b, preferred_element_type=jnp.float32)
    weights = (within * gram).astype(jnp.bfloat16)
    grad_c = jnp.einsum("hts,sn->tn", weights, b_block, preferred_element_type=jnp.float32)
    grad_c = grad_c + jnp.einsum("th,thp,hnp->tn", from_start, upstream_float, state_in, precision=lax.Precision.HIGHEST)
    grad_b = jnp.einsum("hts,tn->sn", weights, c_block, preferred_element_type=jnp.float32)
    grad_b = grad_b + jnp.einsum("th,thp,hnp->tn", to_end, values_float, adjoint_in, precision=lax.Precision.HIGHEST)
    return grad_values.reshape(TOK_DEV, INNER), grad_b, grad_c


def reference(inputs, w_in, b_in, c_in, log_decay, skip, d_out):
    blocks = SEQUENCE_LENGTH // TOK_DEV
    values = jnp.dot(inputs, w_in, preferred_element_type=jnp.float32).astype(jnp.bfloat16)
    values_blocks = values.reshape(blocks, TOK_DEV, ATTENTION_UNITS, HEAD_DIM)
    upstream_blocks = d_out.reshape(blocks, TOK_DEV, ATTENTION_UNITS, HEAD_DIM)
    b_blocks = b_in.reshape(blocks, TOK_DEV, STATE)
    c_blocks = c_in.reshape(blocks, TOK_DEV, STATE)
    decay_blocks = log_decay.reshape(blocks, TOK_DEV, ATTENTION_UNITS)
    block_decay, state_ends, adjoint_starts = lax.map(block_ends, (values_blocks, upstream_blocks, b_blocks, c_blocks, decay_blocks))

    def carry_step(carried, item):
        decay_item, hidden_entry = item
        return decay_item[:, None, None] * carried + hidden_entry, carried

    zero_state = jnp.zeros((ATTENTION_UNITS, STATE, HEAD_DIM), jnp.float32)
    unused_a, states_in = lax.scan(carry_step, zero_state, (block_decay, state_ends))
    unused_b, incoming_cotangents = lax.scan(carry_step, zero_state, (block_decay, adjoint_starts), reverse=True)

    def with_skip(packed):
        return block_grads_skip(packed, skip)

    grad_values, grad_b, grad_c = lax.map(with_skip, (values_blocks, upstream_blocks, b_blocks, c_blocks, decay_blocks, states_in, incoming_cotangents))
    grad_values = grad_values.reshape(SEQUENCE_LENGTH, INNER)
    d_w = lax.dot_general(inputs, grad_values, (((0,), (0,)), ((), ())), preferred_element_type=jnp.float32)
    return d_w, grad_b.reshape(SEQUENCE_LENGTH, STATE), grad_c.reshape(SEQUENCE_LENGTH, STATE)
```

```python
import functools

import jax
import jax.numpy as jnp
from jax import lax
from jax.experimental import pallas as pl
from jax.experimental.pallas import tpu as pltpu
from jax.sharding import PartitionSpec as P

F32 = jnp.float32
BF16 = jnp.bfloat16
MESH = pl.DeviceIdType.MESH
HIGHEST = lax.Precision.HIGHEST
LANES = 128
PLAIN = ((1,), (0,))
SECOND_T = ((1,), (1,))


def dot(a, b, dims=PLAIN, precision=None):
    return lax.dot_general(a, b, (dims, ((), ())), precision=precision, preferred_element_type=F32)


def split(x):
    high = x.astype(BF16)
    return high, (x - high.astype(F32)).astype(BF16)


def dot_split(a, b_pair):
    return dot(a, b_pair[0]) + dot(a, b_pair[1])


def wait_bytes(ref, sem):
    pltpu.make_async_copy(ref, ref, sem).wait()


class Ring:
    def __init__(self, chips, z, core, blocks, ring_send, sib_send, ring_recv, sib_recv):
        self.chips, self.z, self.core, self.blocks = chips, z, core, blocks
        self.ring_send, self.sib_send = ring_send, sib_send
        self.ring_recv, self.sib_recv = ring_recv, sib_recv
        self.half = chips // 2
        up, down = lax.rem(z + 1, chips), lax.rem(z + chips - 1, chips)
        self.up, self.down = 2 * up, 2 * down + 1
        self.next = jnp.where(core == 0, self.up, self.down)
        self.sibling = 2 * z + 1 - core
        self.mine = 2 * z + core

    def copy(self, block, to, send, recv):
        return pltpu.make_async_remote_copy(
            src_ref=self.blocks.at[block],
            dst_ref=self.blocks.at[block],
            send_sem=send,
            recv_sem=recv,
            device_id={"ctx": to},
            device_id_type=MESH,
        )

    def begin(self):
        self.copy(self.mine, self.up, self.ring_send, self.ring_recv.at[1, self.core]).start()
        self.copy(self.mine, self.down, self.ring_send, self.ring_recv.at[1, self.core]).start()
        self.copy(self.mine, self.sibling, self.sib_send, self.sib_recv.at[0, 0]).start()

    def source(self, k):
        back = lax.rem(self.z - k + self.chips, self.chips)
        ahead = lax.rem(self.z + k, self.chips)
        return jnp.where(self.core == 0, back, ahead)

    def sibling_source(self, k):
        back = lax.rem(self.z - k + self.chips, self.chips)
        ahead = lax.rem(self.z + k, self.chips)
        return jnp.where(self.core == 0, ahead, back)

    def step(self, k):
        if k > self.half:
            return
        base = 2 * self.source(k)
        if k == self.half:
            block = base + self.core
            wait_bytes(self.blocks.at[block], self.ring_recv.at[k, 0])
            self.copy(block, self.sibling, self.sib_send, self.sib_recv.at[k, 0]).start()
            return
        for h in range(2):
            wait_bytes(self.blocks.at[base + h], self.ring_recv.at[k, h])
            if k + 1 < self.half:
                self.copy(base + h, self.next, self.ring_send, self.ring_recv.at[k + 1, h]).start()
            self.copy(base + h, self.sibling, self.sib_send, self.sib_recv.at[k, h]).start()
        if k + 1 == self.half:
            self.copy(base + self.core, self.next, self.ring_send, self.ring_recv.at[k + 1, 0]).start()

    def arrived(self, k):
        if k == 0 or k == self.half:
            wait_bytes(self.blocks.at[0], self.sib_recv.at[k, 0])
        else:
            for h in range(2):
                wait_bytes(self.blocks.at[h], self.sib_recv.at[k, h])

    def finish(self):
        wait_bytes(self.blocks.at[pl.ds(0, self.chips - 1)], self.ring_send)
        wait_bytes(self.blocks.at[pl.ds(0, self.chips)], self.sib_send)


class Carry:
    def __init__(self, chips, z, core, worker, start, everything, found, into, sems):
        self.chips, self.z, self.core, self.worker = chips, z, core, worker
        self.start, self.everything, self.found, self.into = start, everything, found, into
        self.send1, self.recv1, self.send2, self.recv2 = [sems.at[i] for i in range(4)]
        self.mine = 2 * z + core

    def put(self, state, decay):
        slices, rows = self.chips, self.start.shape[1] - 8
        for half in range(2):
            part = state[:, half * LANES : (half + 1) * LANES]
            self.start[pl.ds(half * slices // 2, slices // 2), pl.ds(0, rows), :] = part.reshape(
                slices // 2, rows, LANES
            )
            wide = jnp.broadcast_to(decay[:, half * LANES : (half + 1) * LANES], (8, LANES))
            self.start[pl.ds(half * slices // 2, slices // 2), pl.ds(rows, 8), :] = jnp.broadcast_to(
                wide[None], (slices // 2, 8, LANES)
            )

    def send(self):
        def to(k, carry):
            chip = lax.rem(self.z + k, self.chips)
            pltpu.make_async_remote_copy(
                src_ref=self.start.at[chip],
                dst_ref=self.everything.at[self.mine],
                send_sem=self.send1,
                recv_sem=self.recv1,
                device_id={"ctx": 2 * chip + self.worker},
                device_id_type=MESH,
            ).start()
            return carry

        lax.fori_loop(1, self.chips, to, 0)

        @pl.when(self.core == self.worker)
        def _():
            pltpu.make_async_copy(
                self.start.at[self.z], self.everything.at[self.mine], self.recv1
            ).start()

        @pl.when(self.core != self.worker)
        def _():
            pltpu.make_async_remote_copy(
                src_ref=self.start.at[self.z],
                dst_ref=self.everything.at[self.mine],
                send_sem=self.send1,
                recv_sem=self.recv1,
                device_id={"ctx": 2 * self.z + self.worker},
                device_id_type=MESH,
            ).start()

    def work(self, reverse):
        count, rows = 2 * self.chips, self.start.shape[1] - 8

        @pl.when(self.core == self.worker)
        def _():
            wait_bytes(self.everything, self.recv1)

            def step(k, before):
                at = count - 1 - k if reverse else k
                self.found[at] = before.astype(BF16)
                decay = self.everything[at, pl.ds(rows, 8), :]
                state = self.everything[at, pl.ds(0, rows), :]
                wide = jnp.broadcast_to(decay[0:1, :], (rows, LANES))
                return wide * before + state

            lax.fori_loop(0, count, step, jnp.zeros((rows, LANES), F32))

            def to(k, carry):
                there = lax.rem(self.mine + k, count)
                pltpu.make_async_remote_copy(
                    src_ref=self.found.at[there],
                    dst_ref=self.into.at[self.z],
                    send_sem=self.send2,
                    recv_sem=self.recv2,
                    device_id={"ctx": there},
                    device_id_type=MESH,
                ).start()
                return carry

            lax.fori_loop(1, count, to, 0)
            pltpu.make_async_copy(
                self.found.at[self.mine], self.into.at[self.z], self.recv2
            ).start()

    def result(self):
        wait_bytes(self.into, self.recv2)
        slices = self.chips
        halves = [
            self.into[pl.ds(half * slices // 2, slices // 2)].reshape(LANES, LANES) for half in range(2)
        ]
        return jnp.concatenate(halves, axis=1)

    def finish(self):
        @pl.when(self.core == self.worker)
        def _():
            wait_bytes(self.start.at[pl.ds(0, self.chips - 1)], self.send1)
            wait_bytes(self.found.at[pl.ds(0, 2 * self.chips - 1)], self.send2)

        @pl.when(self.core != self.worker)
        def _():
            wait_bytes(self.start, self.send1)


class Total:
    def __init__(self, peers, tp, part, taken, share, full, sems):
        self.peers, self.tp = peers, tp
        self.part, self.taken, self.share, self.full = part, taken, share, full
        self.send1, self.recv1, self.send2, self.recv2 = [sems.at[i] for i in range(4)]

    def send(self, value):
        self.part[...] = value.reshape(self.part.shape)

        def to(k, carry):
            there = lax.rem(self.tp + k, self.peers)
            pltpu.make_async_remote_copy(
                src_ref=self.part.at[there],
                dst_ref=self.taken.at[self.tp],
                send_sem=self.send1,
                recv_sem=self.recv1,
                device_id={"tp": there},
                device_id_type=MESH,
            ).start()
            return carry

        lax.fori_loop(1, self.peers, to, 0)
        pltpu.make_async_copy(self.part.at[self.tp], self.taken.at[self.tp], self.recv1).start()

    def add(self):
        wait_bytes(self.taken, self.recv1)
        total = self.taken[0]
        for k in range(1, self.peers):
            total = total + self.taken[k]
        self.share[...] = total

        def to(k, carry):
            there = lax.rem(self.tp + k, self.peers)
            pltpu.make_async_remote_copy(
                src_ref=self.share,
                dst_ref=self.full.at[self.tp],
                send_sem=self.send2,
                recv_sem=self.recv2,
                device_id={"tp": there},
                device_id_type=MESH,
            ).start()
            return carry

        lax.fori_loop(1, self.peers, to, 0)
        pltpu.make_async_copy(self.share, self.full.at[self.tp], self.recv2).start()

    def result(self):
        wait_bytes(self.full, self.recv2)
        return self.full[...].reshape(LANES, LANES)

    def finish(self):
        wait_bytes(self.part.at[pl.ds(0, self.peers - 1)], self.send1)
        wait_bytes(self.full.at[pl.ds(0, self.peers - 1)], self.send2)


def kernel(
    chips, peers,
    inputs, w, b_ref, c_ref, ld_ref, skip, dout_ref,
    dw_ref, db_ref, dc_ref,
    gw, gg, cols,
    a_start, a_all, a_found, a_into,
    s_start, s_all, s_found, s_into,
    b_part, b_taken, b_share, b_full,
    c_part, c_taken, c_share, c_full,
    ring_send, ring_recv, sib_recv, carry_sems, total_sems, cols_sems,
):
    ctx, tp = lax.axis_index("ctx"), lax.axis_index("tp")
    devices = 2 * chips
    z, core = lax.div(ctx, 2), lax.rem(ctx, 2)
    heads = 4

    barrier = pltpu.get_barrier_semaphore()

    def greet_ctx(k, carry):
        pl.semaphore_signal(
            barrier, inc=1, device_id={"ctx": lax.rem(ctx + k, devices)}, device_id_type=MESH
        )
        return carry

    def greet_tp(k, carry):
        pl.semaphore_signal(
            barrier, inc=1, device_id={"tp": lax.rem(tp + k, peers)}, device_id_type=MESH
        )
        return carry

    lax.fori_loop(1, devices, greet_ctx, 0)
    lax.fori_loop(1, peers, greet_tp, 0)

    ring_w = Ring(chips, z, core, gw, ring_send.at[0], ring_send.at[1], ring_recv.at[0], sib_recv.at[0])
    ring_g = Ring(chips, z, core, gg, ring_send.at[2], ring_send.at[3], ring_recv.at[1], sib_recv.at[1])
    adjoint = Carry(chips, z, core, 0, a_start, a_all, a_found, a_into, carry_sems.at[0])
    state = Carry(chips, z, core, 1, s_start, s_all, s_found, s_into, carry_sems.at[1])
    total_b = Total(peers, tp, b_part, b_taken, b_share, b_full, total_sems.at[0])
    total_c = Total(peers, tp, c_part, c_taken, c_share, c_full, total_sems.at[1])

    gw[ctx] = w[...]
    rows = lax.broadcasted_iota(jnp.int32, (LANES, LANES), 0)
    lanes = lax.broadcasted_iota(jnp.int32, (LANES, LANES), 1)
    lower = (rows >= lanes).astype(F32)
    first = lanes < LANES // 2
    decay_log = ld_ref[...]
    wide_log = jnp.concatenate(
        [
            jnp.where(first, decay_log[:, 2 * q : 2 * q + 1], decay_log[:, 2 * q + 1 : 2 * q + 2])
            for q in range(2)
        ],
        axis=1,
    )
    cumulative = dot(lower, wide_log, precision=HIGHEST)
    block_log = cumulative[LANES - 1 : LANES, :]
    block_decay = jnp.exp(block_log)
    to_end = jnp.exp(block_log - cumulative)
    from_start = jnp.exp(cumulative)
    b, c, dout = b_ref[...], c_ref[...], dout_ref[...]
    b_t = b.astype(F32).T.astype(BF16)
    c_t = c.astype(F32).T.astype(BF16)
    dout_wide = dout.astype(F32)
    started = split(from_start * dout_wide)
    adjoint.put(dot_split(c_t, started), block_decay)

    pl.semaphore_wait(barrier, devices - 1 + peers - 1)

    ring_w.begin()
    adjoint.send()
    ring_w.step(1)

    share = 2 * LANES // peers
    cols_send1, cols_recv1, cols_send2, cols_recv2 = [cols_sems.at[i] for i in range(4)]
    cols_core = lax.div(tp * share, LANES)
    cols_row = pl.multiple_of(lax.rem(tp * share, LANES), share)

    def cols_at(device):
        return inputs.at[pl.ds(cols_row, share), pl.ds(pl.multiple_of(device * LANES, LANES), LANES)]

    @pl.when(core == cols_core)
    def _():
        def to(k, carry):
            there = lax.rem(ctx + k, devices)
            pltpu.make_async_remote_copy(
                src_ref=cols_at(there),
                dst_ref=cols.at[z, tp],
                send_sem=cols_send1,
                recv_sem=cols_recv1,
                device_id={"ctx": there},
                device_id_type=MESH,
            ).start()
            return carry

        lax.fori_loop(1, devices, to, 0)
        pltpu.make_async_copy(cols_at(ctx), cols.at[z, tp], cols_recv1).start()

    ring_w.step(2)
    adjoint.work(True)
    ring_w.step(3)

    def project(total, chip):
        at = pl.multiple_of(chip * 2 * LANES, 2 * LANES)
        block = gw[pl.ds(2 * chip, 2)].reshape(2 * LANES, -1)
        return total + dot(inputs[:, pl.ds(at, 2 * LANES)], block)

    projected = jnp.zeros((LANES, 2 * LANES), F32)
    for k in (1, 2):
        projected = project(projected, ring_w.source(k))

    scores_t = dot(b, c, SECOND_T)
    later = lanes >= rows
    within, within_t = [], []
    for h in range(heads):
        q, side = h // 2, (h % 2) * (LANES // 2)
        wide = cumulative[:, q * LANES : (q + 1) * LANES]
        column = wide[:, side : side + 1]
        row = wide.T[side : side + 1, :]
        within.append(jnp.where(rows >= lanes, jnp.exp(jnp.where(rows >= lanes, column - row, 0.0)), 0.0))
        within_t.append(jnp.where(later, jnp.exp(jnp.where(later, row - column, 0.0)), 0.0))
    local = []
    for q in range(2):
        pair = dout[:, q * LANES : (q + 1) * LANES]
        sides = [dot((within_t[2 * q + i] * scores_t).astype(BF16), pair) for i in range(2)]
        scale = jnp.where(first, skip[2 * q], skip[2 * q + 1])
        local.append(jnp.where(first, sides[0], sides[1]) + scale * pair.astype(F32))
    local = jnp.concatenate(local, axis=1)

    ring_w.step(4)
    adjoint_in = adjoint.result()
    grad_values = local + to_end * dot(b, adjoint_in)
    gg[ctx] = grad_values.astype(BF16)
    ring_g.begin()
    ring_w.step(5)

    wait_bytes(cols.at[:, tp], cols_recv1)

    def cols_to(k, carry):
        there = lax.rem(tp + k, peers)
        pltpu.make_async_remote_copy(
            src_ref=cols.at[:, tp],
            dst_ref=cols.at[:, tp],
            send_sem=cols_send2,
            recv_sem=cols_recv2,
            device_id={"tp": there},
            device_id_type=MESH,
        ).start()
        return carry

    lax.fori_loop(1, peers, cols_to, 0)

    ring_g.step(1)
    for k in range(6, chips // 2 + 1):
        ring_w.step(k)
    ring_g.step(2)

    ring_w.arrived(0)
    projected = project(projected, z)
    for k in range(1, chips // 2):
        ring_w.arrived(k)
        projected = project(projected, ring_w.sibling_source(k))
        if k > 2:
            projected = project(projected, ring_w.source(k))
    ring_w.arrived(chips // 2)
    projected = project(projected, ring_w.source(chips // 2))
    values = projected.astype(BF16)
    ended = split(to_end * values.astype(F32))
    state.put(dot_split(b_t, ended), block_decay)
    state.send()
    ring_g.step(3)

    d_b = dot(ended[0], adjoint_in, SECOND_T) + dot(ended[1], adjoint_in, SECOND_T)
    d_c = jnp.zeros((LANES, LANES), F32)
    for h in range(heads):
        q = h // 2
        mine = first if h % 2 == 0 else jnp.logical_not(first)
        part = values[:, q * LANES : (q + 1) * LANES]
        part = jnp.where(mine, part.astype(F32), 0.0).astype(BF16)
        pair = dout[:, q * LANES : (q + 1) * LANES]
        weights = (within[h] * dot(pair, part, SECOND_T)).astype(BF16)
        weights_t = (within_t[h] * dot(part, pair, SECOND_T)).astype(BF16)
        d_c = d_c + dot(weights, b)
        d_b = d_b + dot(weights_t, c)
    total_b.send(d_b)
    state.work(False)
    ring_g.step(4)
    total_b.add()
    ring_g.step(5)
    state_in = state.result()
    d_c = d_c + dot(started[0], state_in, SECOND_T) + dot(started[1], state_in, SECOND_T)
    total_c.send(d_c)
    for k in range(6, chips // 2):
        ring_g.step(k)
    total_c.add()
    for k in range(max(6, chips // 2), chips // 2 + 1):
        ring_g.step(k)

    wait_bytes(cols.at[:, pl.ds(0, peers - 1)], cols_recv2)

    def project_back(total, chip):
        return total + dot(
            cols[chip].reshape(2 * LANES, LANES).astype(F32).T.astype(BF16),
            gg[pl.ds(2 * chip, 2)].reshape(2 * LANES, -1),
        )

    ring_g.arrived(0)
    grad_w = project_back(jnp.zeros((LANES, 2 * LANES), F32), z)
    for k in range(1, chips // 2):
        grad_w = project_back(grad_w, ring_g.source(k))
        ring_g.arrived(k)
        grad_w = project_back(grad_w, ring_g.sibling_source(k))
    ring_g.arrived(chips // 2)
    dw_ref[...] = project_back(grad_w, ring_g.source(chips // 2))
    db_ref[...] = total_b.result()
    dc_ref[...] = total_c.result()

    ring_w.finish()
    ring_g.finish()
    adjoint.finish()
    state.finish()
    total_b.finish()
    total_c.finish()

    @pl.when(core == cols_core)
    def _():
        wait_bytes(inputs.at[pl.ds(0, share), pl.ds(0, (devices - 1) * LANES)], cols_send1)

    wait_bytes(cols.at[:, pl.ds(0, peers - 1)], cols_send2)


def solution(mesh):
    devices, peers = mesh.shape["ctx"], mesh.shape["tp"]
    chips = devices // 2

    def per_device(inputs, w_in, b_in, c_in, log_decay, skip, d_out):
        tokens, width = d_out.shape
        rows = LANES // (chips // 2)
        vmem = pl.BlockSpec(memory_space=pltpu.VMEM)
        carry_scratch = [
            pltpu.VMEM((chips, rows + 8, LANES), F32),
            pltpu.VMEM((devices, rows + 8, LANES), F32),
            pltpu.VMEM((devices, rows, LANES), BF16),
            pltpu.VMEM((chips, rows, LANES), BF16),
        ]
        total_scratch = [
            pltpu.VMEM((peers, tokens // peers, LANES), F32),
            pltpu.VMEM((peers, tokens // peers, LANES), F32),
            pltpu.VMEM((tokens // peers, LANES), F32),
            pltpu.VMEM((peers, tokens // peers, LANES), F32),
        ]
        half = chips // 2
        return pl.pallas_call(
            functools.partial(kernel, chips, peers),
            out_shape=(
                jax.ShapeDtypeStruct(w_in.shape, F32),
                jax.ShapeDtypeStruct(b_in.shape, F32),
                jax.ShapeDtypeStruct(c_in.shape, F32),
            ),
            in_specs=[vmem] * 5 + [pl.BlockSpec(memory_space=pltpu.SMEM), vmem],
            out_specs=(vmem, vmem, vmem),
            scratch_shapes=[
                pltpu.VMEM((devices, tokens, width), BF16),
                pltpu.VMEM((devices, tokens, width), BF16),
                pltpu.VMEM((chips, peers, 2 * tokens // peers, LANES), BF16),
            ]
            + carry_scratch * 2
            + total_scratch * 2
            + [
                pltpu.SemaphoreType.DMA((4,)),
                pltpu.SemaphoreType.DMA((2, half + 1, 2)),
                pltpu.SemaphoreType.DMA((2, half + 1, 2)),
                pltpu.SemaphoreType.DMA((2, 4)),
                pltpu.SemaphoreType.DMA((2, 4)),
                pltpu.SemaphoreType.DMA((4,)),
            ],
            compiler_params=pltpu.CompilerParams(
                collective_id=0, has_side_effects=True, vmem_limit_bytes=48 * 1024 * 1024
            ),
        )(inputs, w_in, b_in, c_in, log_decay, skip, d_out)

    return jax.shard_map(
        per_device,
        mesh=mesh,
        in_specs=(
            P("ctx", None),
            P("ctx", "tp"),
            P("ctx", None),
            P("ctx", None),
            P("ctx", "tp"),
            P("tp"),
            P("ctx", "tp"),
        ),
        out_specs=(P("ctx", "tp"), P("ctx", None), P("ctx", None)),
        check_vma=False,
    )
```

```python
import functools

import jax
import jax.numpy as jnp
from jax import lax
from jax.experimental import pallas as pl
from jax.experimental.pallas import tpu as pltpu
from jax.sharding import PartitionSpec as P

F32 = jnp.float32
BF16 = jnp.bfloat16
MESH = pl.DeviceIdType.MESH
HIGHEST = lax.Precision.HIGHEST
LANES = 128
PLAIN = ((1,), (0,))
SECOND_T = ((1,), (1,))


def dot(a, b, dims=PLAIN, precision=None):
    return lax.dot_general(a, b, (dims, ((), ())), precision=precision, preferred_element_type=F32)


def split(x):
    high = x.astype(BF16)
    return high, (x - high.astype(F32)).astype(BF16)


def dot_split(a, b_pair):
    return dot(a, b_pair[0]) + dot(a, b_pair[1])


def carried(a_pair, b_pair):
    return sum(dot(a_pair[i], b_pair[j], SECOND_T) for i, j in ((0, 0), (0, 1), (1, 0)))


def wait_bytes(ref, sem):
    pltpu.make_async_copy(ref, ref, sem).wait()


def far_first(place, i, count):
    aside = lax.div(i + 1, 2)
    return lax.rem(place + count // 2 + jnp.where(lax.rem(i, 2) == 1, count - aside, aside), count)


class Ring:
    def __init__(self, chips, stride, z, core, blocks, ring_send, sib_send, ring_recv, sib_recv):
        self.chips, self.stride, self.half = chips, stride, chips // 2
        self.z, self.core, self.blocks = z, core, blocks
        self.ring_send, self.sib_send = ring_send, sib_send
        self.ring_recv, self.sib_recv = ring_recv, sib_recv
        self.sibling, self.mine = 2 * z + 1 - core, 2 * z + core

    def copy(self, block, to, send, recv):
        pltpu.make_async_remote_copy(
            src_ref=self.blocks.at[block],
            dst_ref=self.blocks.at[block],
            send_sem=send,
            recv_sem=recv,
            device_id={"ctx": to},
            device_id_type=MESH,
        ).start()

    def back(self, k):
        return lax.rem(self.z + (self.chips - k), self.chips)

    def ahead(self, k):
        return lax.rem(self.z + k, self.chips)

    def source(self, k):
        return jnp.where(self.core == 0, self.back(k), self.ahead(k))

    def sibling_source(self, k):
        return jnp.where(self.core == 0, self.ahead(k), self.back(k))

    def begin(self):
        for s in range(self.stride, 0, -1):
            recv = self.ring_recv.at[s, self.core]
            self.copy(self.mine, 2 * self.ahead(s), self.ring_send, recv)
            self.copy(self.mine, 2 * self.back(s) + 1, self.ring_send, recv)
        self.copy(self.mine, self.sibling, self.sib_send, self.sib_recv.at[0, 0])

    def step(self, k):
        if k > self.half:
            return
        base = 2 * self.source(k)
        if k == self.half:
            block = base + self.core
            wait_bytes(self.blocks.at[block], self.ring_recv.at[k, 0])
            self.copy(block, self.sibling, self.sib_send, self.sib_recv.at[k, 0])
            return
        onward = [s for s in range(self.stride, 0, -1) if k % self.stride == 0 and k + s <= self.half]
        for h in range(2):
            wait_bytes(self.blocks.at[base + h], self.ring_recv.at[k, h])
            for s in onward:
                if k + s < self.half:
                    to = 2 * self.sibling_source(s) + self.core
                    self.copy(base + h, to, self.ring_send, self.ring_recv.at[k + s, h])
            self.copy(base + h, self.sibling, self.sib_send, self.sib_recv.at[k, h])
        for s in onward:
            if k + s == self.half:
                to = 2 * self.sibling_source(s) + self.core
                self.copy(base + self.core, to, self.ring_send, self.ring_recv.at[k + s, 0])

    def arrived(self, k):
        if k == 0 or k == self.half:
            wait_bytes(self.blocks.at[0], self.sib_recv.at[k, 0])
        else:
            for h in range(2):
                wait_bytes(self.blocks.at[h], self.sib_recv.at[k, h])

    def finish(self):
        wait_bytes(self.blocks.at[pl.ds(0, self.chips - 1)], self.ring_send)
        wait_bytes(self.blocks.at[pl.ds(0, self.chips)], self.sib_send)


class Carry:
    def __init__(self, chips, z, core, near, decays, refs, sems):
        self.chips, self.z, self.core, self.near = chips, z, core, near
        self.start, self.peer, self.joined, self.everything, self.found, self.into = refs
        self.peer_send, self.peer_recv, self.send1, self.recv1, self.send2, self.send3, self.recv2 = [
            sems.at[i] for i in range(7)
        ]
        self.rows = self.into.shape[1]
        self.decays = self.everything if decays is None else decays
        self.sent = self.everything.shape[1]

    def put(self, state, decay):
        slices, rows = self.chips, self.rows
        for half in range(2):
            at = pl.ds(half * slices // 2, slices // 2)
            part = state[:, half * LANES : (half + 1) * LANES]
            self.start[at, pl.ds(0, rows), :] = part.reshape(slices // 2, rows, LANES)
            wide = jnp.broadcast_to(decay[:, half * LANES : (half + 1) * LANES], (8, LANES))
            self.start[at, pl.ds(rows, 8), :] = jnp.broadcast_to(wide[None], (slices // 2, 8, LANES))

    def hand(self):
        @pl.when(self.core == self.near)
        def _():
            pltpu.make_async_remote_copy(
                src_ref=self.start,
                dst_ref=self.peer,
                send_sem=self.peer_send,
                recv_sem=self.peer_recv,
                device_id={"ctx": 2 * self.z + 1 - self.near},
                device_id_type=MESH,
            ).start()
            self.peer[:, pl.ds(0, self.rows), :] = jnp.zeros((self.chips, self.rows, LANES), F32)
            self.peer[:, pl.ds(self.rows, 8), :] = jnp.ones((self.chips, 8, LANES), F32)

    def send(self):
        rows = self.rows

        @pl.when(self.core != self.near)
        def _():
            wait_bytes(self.peer, self.peer_recv)
            decay = self.start[:, rows : rows + 1, :]
            self.joined[:, pl.ds(0, rows), :] = self.start[:, 0:rows, :] + decay * self.peer[:, 0:rows, :]
            self.joined[:, pl.ds(rows, 8), :] = decay * self.peer[:, rows : rows + 8, :]

            def copy(chip):
                return dict(
                    src_ref=self.joined.at[chip, pl.ds(0, self.sent)],
                    dst_ref=self.everything.at[self.z],
                )

            def to(i, carry):
                chip = far_first(self.z, i, self.chips)
                pltpu.make_async_remote_copy(
                    **copy(chip),
                    send_sem=self.send1,
                    recv_sem=self.recv1,
                    device_id={"ctx": 2 * chip},
                    device_id_type=MESH,
                ).start()
                return carry

            lax.fori_loop(0, self.chips - 1, to, 0)
            if self.near == 1:
                pltpu.make_async_copy(*copy(self.z).values(), self.recv1).start()
            else:
                pltpu.make_async_remote_copy(
                    **copy(self.z),
                    send_sem=self.send1,
                    recv_sem=self.recv1,
                    device_id={"ctx": 2 * self.z},
                    device_id_type=MESH,
                ).start()

    def work(self):
        count, rows = self.chips, self.rows

        @pl.when(self.core == 0)
        def _():
            wait_bytes(self.everything, self.recv1)
            before = jnp.zeros((rows, LANES), F32)
            for k in range(count):
                at = count - 1 - k if self.near == 1 else k
                self.found[at] = before.astype(BF16)
                decay = jnp.broadcast_to(self.decays[at, rows : rows + 1, :], (rows, LANES))
                before = decay * before + self.everything[at, 0:rows, :]

            def copy(chip, core):
                return pltpu.make_async_remote_copy(
                    src_ref=self.found.at[chip],
                    dst_ref=self.into.at[self.z],
                    send_sem=self.send3 if core else self.send2,
                    recv_sem=self.recv2,
                    device_id={"ctx": 2 * chip + core},
                    device_id_type=MESH,
                )

            def to(i, carry):
                chip = far_first(self.z, i, count)
                copy(chip, 0).start()
                copy(chip, 1).start()
                return carry

            lax.fori_loop(0, count - 1, to, 0)
            copy(self.z, 1).start()
            pltpu.make_async_copy(self.found.at[self.z], self.into.at[self.z], self.recv2).start()

    def result(self):
        wait_bytes(self.into, self.recv2)
        halves = []
        for half in range(2):
            at = pl.ds(half * self.chips // 2, self.chips // 2)
            peer = self.peer[at]
            decay = peer[:, self.rows : self.rows + 1, :]
            part = decay * self.into[at].astype(F32) + peer[:, 0 : self.rows, :]
            halves.append(part.reshape(LANES, LANES))
        return split(jnp.concatenate(halves, axis=1))

    def finish(self):
        @pl.when(self.core == self.near)
        def _():
            wait_bytes(self.start, self.peer_send)

        @pl.when(self.core != self.near)
        def _():
            wait_bytes(self.joined.at[pl.ds(0, self.chips - self.near), pl.ds(0, self.sent)], self.send1)

        @pl.when(self.core == 0)
        def _():
            wait_bytes(self.found.at[pl.ds(0, self.chips - 1)], self.send2)
            wait_bytes(self.found, self.send3)


class Total:
    def __init__(self, peers, tp, part, taken, share, full, sems):
        self.peers, self.tp = peers, tp
        self.part, self.taken, self.share, self.full = part, taken, share, full
        self.send1, self.recv1, self.send2, self.recv2 = [sems.at[i] for i in range(4)]

    def send(self, value):
        self.part[...] = value.reshape(self.part.shape)

        def to(k, carry):
            there = lax.rem(self.tp + k, self.peers)
            pltpu.make_async_remote_copy(
                src_ref=self.part.at[there],
                dst_ref=self.taken.at[self.tp],
                send_sem=self.send1,
                recv_sem=self.recv1,
                device_id={"tp": there},
                device_id_type=MESH,
            ).start()
            return carry

        lax.fori_loop(1, self.peers, to, 0)
        pltpu.make_async_copy(self.part.at[self.tp], self.taken.at[self.tp], self.recv1).start()

    def add(self):
        wait_bytes(self.taken, self.recv1)
        total = self.taken[0]
        for k in range(1, self.peers):
            total = total + self.taken[k]
        self.share[...] = total

        def to(k, carry):
            there = lax.rem(self.tp + k, self.peers)
            pltpu.make_async_remote_copy(
                src_ref=self.share,
                dst_ref=self.full.at[self.tp],
                send_sem=self.send2,
                recv_sem=self.recv2,
                device_id={"tp": there},
                device_id_type=MESH,
            ).start()
            return carry

        lax.fori_loop(1, self.peers, to, 0)
        pltpu.make_async_copy(self.share, self.full.at[self.tp], self.recv2).start()

    def result(self):
        wait_bytes(self.full, self.recv2)
        return self.full[...].reshape(LANES, LANES)

    def finish(self):
        wait_bytes(self.part.at[pl.ds(0, self.peers - 1)], self.send1)
        wait_bytes(self.full.at[pl.ds(0, self.peers - 1)], self.send2)


class Columns:
    def __init__(self, chips, peers, ctx, z, core, tp, inputs, cols, sems):
        self.devices, self.peers = 2 * chips, peers
        self.ctx, self.z, self.core, self.tp = ctx, z, core, tp
        self.inputs, self.cols = inputs, cols
        self.send1, self.recv1, self.send2, self.recv2 = [sems.at[i] for i in range(4)]
        self.share = 2 * LANES // peers
        self.sender = lax.div(tp * self.share, LANES)
        self.row = pl.multiple_of(lax.rem(tp * self.share, LANES), self.share)

    def block(self, device):
        at = pl.multiple_of(device * LANES, LANES)
        return self.inputs.at[pl.ds(self.row, self.share), pl.ds(at, LANES)]

    def send(self):
        @pl.when(self.core == self.sender)
        def _():
            def to(k, carry):
                there = lax.rem(self.ctx + k, self.devices)
                pltpu.make_async_remote_copy(
                    src_ref=self.block(there),
                    dst_ref=self.cols.at[self.z, self.tp],
                    send_sem=self.send1,
                    recv_sem=self.recv1,
                    device_id={"ctx": there},
                    device_id_type=MESH,
                ).start()
                return carry

            lax.fori_loop(1, self.devices, to, 0)
            pltpu.make_async_copy(
                self.block(self.ctx), self.cols.at[self.z, self.tp], self.recv1
            ).start()

    def spread(self):
        mine = self.cols.at[:, self.tp]
        wait_bytes(mine, self.recv1)

        def to(k, carry):
            there = lax.rem(self.tp + k, self.peers)
            pltpu.make_async_remote_copy(
                src_ref=mine,
                dst_ref=mine,
                send_sem=self.send2,
                recv_sem=self.recv2,
                device_id={"tp": there},
                device_id_type=MESH,
            ).start()
            return carry

        lax.fori_loop(1, self.peers, to, 0)

    def arrived(self):
        wait_bytes(self.cols.at[:, pl.ds(0, self.peers - 1)], self.recv2)

    def finish(self):
        @pl.when(self.core == self.sender)
        def _():
            sent = self.inputs.at[pl.ds(0, self.share), pl.ds(0, (self.devices - 1) * LANES)]
            wait_bytes(sent, self.send1)

        wait_bytes(self.cols.at[:, pl.ds(0, self.peers - 1)], self.send2)


def kernel(
    chips, peers,
    inputs_hbm, w_hbm, b_hbm, c_hbm, ld_hbm, skip, dout_hbm,
    dw_ref, db_ref, dc_ref,
    inputs, b_ref, c_ref, ld_ref, dout_ref,
    gw, gg, cols,
    a_start, a_peer, a_joined, a_all, a_found, a_into,
    s_start, s_peer, s_joined, s_all, s_found, s_into,
    b_part, b_taken, b_share, b_full,
    c_part, c_taken, c_share, c_full,
    ring_send, ring_recv, sib_recv, carry_sems, total_sems, cols_sems, fetch_sems,
):
    ctx, tp = lax.axis_index("ctx"), lax.axis_index("tp")
    devices = 2 * chips
    z, core = lax.div(ctx, 2), lax.rem(ctx, 2)
    heads = 4

    fetches = [
        pltpu.make_async_copy(there, here, fetch_sems.at[i])
        for i, (there, here) in enumerate(
            [
                (ld_hbm, ld_ref),
                (c_hbm, c_ref),
                (dout_hbm, dout_ref),
                (b_hbm, b_ref),
                (w_hbm, gw.at[ctx]),
                (inputs_hbm, inputs),
            ]
        )
    ]
    for fetch in fetches:
        fetch.start()

    barrier = pltpu.get_barrier_semaphore()

    def greet_ctx(k, carry):
        pl.semaphore_signal(
            barrier, inc=1, device_id={"ctx": lax.rem(ctx + k, devices)}, device_id_type=MESH
        )
        return carry

    def greet_tp(k, carry):
        pl.semaphore_signal(
            barrier, inc=1, device_id={"tp": lax.rem(tp + k, peers)}, device_id_type=MESH
        )
        return carry

    lax.fori_loop(1, devices, greet_ctx, 0)
    lax.fori_loop(1, peers, greet_tp, 0)

    ring_w = Ring(
        chips, 2, z, core, gw, ring_send.at[0], ring_send.at[1], ring_recv.at[0], sib_recv.at[0]
    )
    ring_g = Ring(
        chips, 2, z, core, gg, ring_send.at[2], ring_send.at[3], ring_recv.at[1], sib_recv.at[1]
    )
    adjoint = Carry(
        chips, z, core, 1, None, (a_start, a_peer, a_joined, a_all, a_found, a_into), carry_sems.at[0]
    )
    state = Carry(
        chips, z, core, 0, a_all, (s_start, s_peer, s_joined, s_all, s_found, s_into), carry_sems.at[1]
    )
    total_b = Total(peers, tp, b_part, b_taken, b_share, b_full, total_sems.at[0])
    columns = Columns(chips, peers, ctx, z, core, tp, inputs, cols, cols_sems)
    total_c = Total(peers, tp, c_part, c_taken, c_share, c_full, total_sems.at[1])

    rows = lax.broadcasted_iota(jnp.int32, (LANES, LANES), 0)
    lanes = lax.broadcasted_iota(jnp.int32, (LANES, LANES), 1)
    upper = (rows <= lanes).astype(F32)
    first, first_rows = lanes < LANES // 2, rows < LANES // 2
    for fetch in fetches[:4]:
        fetch.wait()
    cumulative_t = []
    for q in range(2):
        pair = [jnp.broadcast_to(ld_ref[2 * q + i : 2 * q + i + 1, :], (LANES, LANES)) for i in range(2)]
        cumulative_t.append(dot(jnp.where(first_rows, pair[0], pair[1]), upper, precision=HIGHEST))
    cumulative = jnp.concatenate([part.T for part in cumulative_t], axis=1)
    block_log = cumulative[LANES - 1 : LANES, :]
    block_decay = jnp.exp(block_log)
    to_end = jnp.exp(block_log - cumulative)
    from_start = jnp.exp(cumulative)
    b, c, dout = b_ref[...], c_ref[...], dout_ref[...]
    b_t = b.astype(F32).T.astype(BF16)
    c_t = c.astype(F32).T.astype(BF16)
    dout_wide = dout.astype(F32)
    started = split(from_start * dout_wide)
    adjoint.put(dot_split(c_t, started), block_decay)

    pl.semaphore_wait(barrier, devices - 1 + peers - 1)
    for fetch in fetches[4:]:
        fetch.wait()

    ring_w.begin()
    adjoint.hand()
    adjoint.send()
    ring_w.step(2)
    ring_w.step(1)
    columns.send()

    def project(total, chip):
        at = pl.multiple_of(chip * 2 * LANES, 2 * LANES)
        block = gw[pl.ds(2 * chip, 2)].reshape(2 * LANES, -1)
        return total + dot(inputs[:, pl.ds(at, 2 * LANES)], block)

    ring_w.step(4)
    ring_w.step(3)
    ring_w.arrived(0)
    projected = project(jnp.zeros((LANES, 2 * LANES), F32), z)
    for k in (1, 2):
        projected = project(projected, ring_w.source(k))
        ring_w.arrived(k)
        projected = project(projected, ring_w.sibling_source(k))
    adjoint.work()
    ring_w.step(6)
    ring_w.step(5)

    scores_t = dot(b, c, SECOND_T)
    later = lanes >= rows
    within, within_t = [], []
    for h in range(heads):
        q, side = h // 2, (h % 2) * (LANES // 2)
        column = cumulative[:, q * LANES + side : q * LANES + side + 1]
        row = cumulative_t[q][side : side + 1, :]
        within.append(jnp.where(rows >= lanes, jnp.exp(jnp.where(rows >= lanes, column - row, 0.0)), 0.0))
        within_t.append(jnp.where(later, jnp.exp(jnp.where(later, row - column, 0.0)), 0.0))
    local = []
    for q in range(2):
        pair = dout[:, q * LANES : (q + 1) * LANES]
        sides = [dot((within_t[2 * q + i] * scores_t).astype(BF16), pair) for i in range(2)]
        scale = jnp.where(first, skip[2 * q], skip[2 * q + 1])
        local.append(jnp.where(first, sides[0], sides[1]) + scale * pair.astype(F32))
    local = jnp.concatenate(local, axis=1)

    columns.spread()
    for k in range(3, chips // 2 - 1):
        projected = project(projected, ring_w.source(k))
        ring_w.arrived(k)
        projected = project(projected, ring_w.sibling_source(k))
    ring_w.step(8)
    ring_w.step(7)

    k = chips // 2 - 1
    projected = project(projected, ring_w.source(k))
    ring_w.arrived(k)
    projected = project(projected, ring_w.sibling_source(k))
    ring_w.arrived(chips // 2)
    projected = project(projected, ring_w.source(chips // 2))
    values = projected.astype(BF16)
    ended = split(to_end * values.astype(F32))
    state.put(dot_split(b_t, ended), block_decay)
    state.hand()

    adjoint_in = adjoint.result()
    grad_values = local + to_end * dot_split(b, adjoint_in)
    gg[ctx] = grad_values.astype(BF16)
    ring_g.begin()
    state.send()

    d_b = carried(ended, adjoint_in)
    d_c = jnp.zeros((LANES, LANES), F32)
    for h in range(heads):
        q = h // 2
        mine = first if h % 2 == 0 else jnp.logical_not(first)
        part = values[:, q * LANES : (q + 1) * LANES]
        part = jnp.where(mine, part.astype(F32), 0.0).astype(BF16)
        pair = dout[:, q * LANES : (q + 1) * LANES]
        weights = (within[h] * dot(pair, part, SECOND_T)).astype(BF16)
        weights_t = (within_t[h] * dot(part, pair, SECOND_T)).astype(BF16)
        d_c = d_c + dot(weights, b)
        d_b = d_b + dot(weights_t, c)
    total_b.send(d_b)
    ring_g.step(2)
    ring_g.step(1)
    ring_g.step(4)
    ring_g.step(3)
    state.work()
    total_b.add()
    ring_g.step(6)
    ring_g.step(5)
    state_in = state.result()
    d_c = d_c + carried(started, state_in)
    total_c.send(d_c)
    ring_g.step(8)
    ring_g.step(7)
    total_c.add()

    columns.arrived()

    def project_back(total, chip):
        return total + dot(
            cols[chip].reshape(2 * LANES, LANES).astype(F32).T.astype(BF16),
            gg[pl.ds(2 * chip, 2)].reshape(2 * LANES, -1),
        )

    ring_g.arrived(0)
    grad_w = project_back(jnp.zeros((LANES, 2 * LANES), F32), z)
    for k in range(1, chips // 2):
        grad_w = project_back(grad_w, ring_g.source(k))
        ring_g.arrived(k)
        grad_w = project_back(grad_w, ring_g.sibling_source(k))
    ring_g.arrived(chips // 2)
    dw_ref[...] = project_back(grad_w, ring_g.source(chips // 2))
    db_ref[...] = total_b.result()
    dc_ref[...] = total_c.result()

    ring_w.finish()
    ring_g.finish()
    adjoint.finish()
    state.finish()
    total_b.finish()
    total_c.finish()
    columns.finish()


def solution(mesh):
    devices, peers = mesh.shape["ctx"], mesh.shape["tp"]
    chips = devices // 2

    def per_device(inputs, w_in, b_in, c_in, log_decay, skip, d_out):
        tokens, width = d_out.shape
        rows = LANES // (chips // 2)
        vmem, hbm = pl.BlockSpec(memory_space=pltpu.VMEM), pl.BlockSpec(memory_space=pltpu.HBM)
        def carry_scratch(sent):
            return [
                pltpu.VMEM((chips, rows + 8, LANES), F32),
                pltpu.VMEM((chips, rows + 8, LANES), F32),
                pltpu.VMEM((chips, rows + 8, LANES), F32),
                pltpu.VMEM((chips, sent, LANES), F32),
                pltpu.VMEM((chips, rows, LANES), BF16),
                pltpu.VMEM((chips, rows, LANES), BF16),
            ]

        total_scratch = [
            pltpu.VMEM((peers, tokens // peers, LANES), F32),
            pltpu.VMEM((peers, tokens // peers, LANES), F32),
            pltpu.VMEM((tokens // peers, LANES), F32),
            pltpu.VMEM((peers, tokens // peers, LANES), F32),
        ]
        half = chips // 2
        return pl.pallas_call(
            functools.partial(kernel, chips, peers),
            out_shape=(
                jax.ShapeDtypeStruct(w_in.shape, F32),
                jax.ShapeDtypeStruct(b_in.shape, F32),
                jax.ShapeDtypeStruct(c_in.shape, F32),
            ),
            in_specs=[hbm] * 5 + [pl.BlockSpec(memory_space=pltpu.SMEM), hbm],
            out_specs=(vmem, vmem, vmem),
            scratch_shapes=[
                pltpu.VMEM(inputs.shape, BF16),
                pltpu.VMEM(b_in.shape, BF16),
                pltpu.VMEM(c_in.shape, BF16),
                pltpu.VMEM(log_decay.shape[::-1], F32),
                pltpu.VMEM(d_out.shape, BF16),
                pltpu.VMEM((devices, tokens, width), BF16),
                pltpu.VMEM((devices, tokens, width), BF16),
                pltpu.VMEM((chips, peers, 2 * tokens // peers, LANES), BF16),
            ]
            + carry_scratch(rows + 8)
            + carry_scratch(rows)
            + total_scratch * 2
            + [
                pltpu.SemaphoreType.DMA((4,)),
                pltpu.SemaphoreType.DMA((2, half + 1, 2)),
                pltpu.SemaphoreType.DMA((2, half + 1, 2)),
                pltpu.SemaphoreType.DMA((2, 7)),
                pltpu.SemaphoreType.DMA((2, 4)),
                pltpu.SemaphoreType.DMA((4,)),
                pltpu.SemaphoreType.DMA((6,)),
            ],
            compiler_params=pltpu.CompilerParams(
                collective_id=0, has_side_effects=True, vmem_limit_bytes=60 * 1024 * 1024
            ),
        )(inputs, w_in, b_in, c_in, log_decay.T, skip, d_out)

    return jax.shard_map(
        per_device,
        mesh=mesh,
        in_specs=(
            P("ctx", None),
            P("ctx", "tp"),
            P("ctx", None),
            P("ctx", None),
            P("ctx", "tp"),
            P("tp"),
            P("ctx", "tp"),
        ),
        out_specs=(P("ctx", "tp"), P("ctx", None), P("ctx", None)),
        check_vma=False,
    )
```

```python
import functools

import jax
import jax.numpy as jnp
from jax import lax
from jax.experimental import pallas as pl
from jax.experimental.pallas import tpu as pltpu
from jax.sharding import PartitionSpec as P

F32 = jnp.float32
BF16 = jnp.bfloat16
MESH = pl.DeviceIdType.MESH
HIGHEST = lax.Precision.HIGHEST
LANES = 128
PLAIN = ((1,), (0,))
SECOND_T = ((1,), (1,))


def dot(a, b, dims=PLAIN, precision=None):
    return lax.dot_general(a, b, (dims, ((), ())), precision=precision, preferred_element_type=F32)


def split(x):
    high = x.astype(BF16)
    return high, (x - high.astype(F32)).astype(BF16)


def dot_split(a, b_pair):
    return dot(a, b_pair[0]) + dot(a, b_pair[1])


def carried(a_pair, b_pair):
    return sum(dot(a_pair[i], b_pair[j], SECOND_T) for i, j in ((0, 0), (0, 1), (1, 0)))


def wait_bytes(ref, sem):
    pltpu.make_async_copy(ref, ref, sem).wait()


def far_first(place, i, count):
    aside = lax.div(i + 1, 2)
    return lax.rem(place + count // 2 + jnp.where(lax.rem(i, 2) == 1, count - aside, aside), count)


class Ring:
    def __init__(self, chips, stride, z, core, blocks, ring_send, sib_send, ring_recv, sib_recv):
        self.chips, self.stride, self.half = chips, stride, chips // 2
        self.z, self.core, self.blocks = z, core, blocks
        self.ring_send, self.sib_send = ring_send, sib_send
        self.ring_recv, self.sib_recv = ring_recv, sib_recv
        self.sibling, self.mine = 2 * z + 1 - core, 2 * z + core

    def copy(self, block, to, send, recv):
        pltpu.make_async_remote_copy(
            src_ref=self.blocks.at[block],
            dst_ref=self.blocks.at[block],
            send_sem=send,
            recv_sem=recv,
            device_id={"ctx": to},
            device_id_type=MESH,
        ).start()

    def back(self, k):
        return lax.rem(self.z + (self.chips - k), self.chips)

    def ahead(self, k):
        return lax.rem(self.z + k, self.chips)

    def source(self, k):
        return jnp.where(self.core == 0, self.back(k), self.ahead(k))

    def sibling_source(self, k):
        return jnp.where(self.core == 0, self.ahead(k), self.back(k))

    def begin(self):
        for s in range(self.stride, 0, -1):
            recv = self.ring_recv.at[s, self.core]
            self.copy(self.mine, 2 * self.ahead(s), self.ring_send, recv)
            self.copy(self.mine, 2 * self.back(s) + 1, self.ring_send, recv)
        self.copy(self.mine, self.sibling, self.sib_send, self.sib_recv.at[0, 0])

    def step(self, k):
        if k > self.half:
            return
        base = 2 * self.source(k)
        if k == self.half:
            block = base + self.core
            wait_bytes(self.blocks.at[block], self.ring_recv.at[k, 0])
            self.copy(block, self.sibling, self.sib_send, self.sib_recv.at[k, 0])
            return
        onward = [s for s in range(self.stride, 0, -1) if k % self.stride == 0 and k + s <= self.half]
        for h in range(2):
            wait_bytes(self.blocks.at[base + h], self.ring_recv.at[k, h])
            for s in onward:
                if k + s < self.half:
                    to = 2 * self.sibling_source(s) + self.core
                    self.copy(base + h, to, self.ring_send, self.ring_recv.at[k + s, h])
            self.copy(base + h, self.sibling, self.sib_send, self.sib_recv.at[k, h])
        for s in onward:
            if k + s == self.half:
                to = 2 * self.sibling_source(s) + self.core
                self.copy(base + self.core, to, self.ring_send, self.ring_recv.at[k + s, 0])

    def arrived(self, k):
        if k == 0 or k == self.half:
            wait_bytes(self.blocks.at[0], self.sib_recv.at[k, 0])
        else:
            for h in range(2):
                wait_bytes(self.blocks.at[h], self.sib_recv.at[k, h])

    def finish(self):
        wait_bytes(self.blocks.at[pl.ds(0, self.chips - 1)], self.ring_send)
        wait_bytes(self.blocks.at[pl.ds(0, self.chips)], self.sib_send)


class Carry:
    def __init__(self, chips, z, core, near, decays, refs, sems):
        self.chips, self.z, self.core, self.near = chips, z, core, near
        self.start, self.peer, self.joined, self.everything, self.found, self.into = refs
        self.peer_send, self.peer_recv, self.send1, self.recv1, self.send2, self.recv2, self.send3, self.recv3 = [
            sems.at[i] for i in range(8)
        ]
        self.rows = self.into.shape[1]
        self.decays = self.everything if decays is None else decays
        self.sent = self.everything.shape[1]

    def put(self, state, decay):
        slices, rows = self.chips, self.rows
        for half in range(2):
            at = pl.ds(half * slices // 2, slices // 2)
            part = state[:, half * LANES : (half + 1) * LANES]
            self.start[at, pl.ds(0, rows), :] = part.reshape(slices // 2, rows, LANES)
            wide = jnp.broadcast_to(decay[:, half * LANES : (half + 1) * LANES], (8, LANES))
            self.start[at, pl.ds(rows, 8), :] = jnp.broadcast_to(wide[None], (slices // 2, 8, LANES))

    def hand(self):
        @pl.when(self.core == self.near)
        def _():
            pltpu.make_async_remote_copy(
                src_ref=self.start,
                dst_ref=self.peer,
                send_sem=self.peer_send,
                recv_sem=self.peer_recv,
                device_id={"ctx": 2 * self.z + 1 - self.near},
                device_id_type=MESH,
            ).start()
            self.peer[:, pl.ds(0, self.rows), :] = jnp.zeros((self.chips, self.rows, LANES), F32)
            self.peer[:, pl.ds(self.rows, 8), :] = jnp.ones((self.chips, 8, LANES), F32)

    def send(self):
        rows = self.rows

        @pl.when(self.core != self.near)
        def _():
            wait_bytes(self.peer, self.peer_recv)
            decay = self.start[:, rows : rows + 1, :]
            self.joined[:, pl.ds(0, rows), :] = self.start[:, 0:rows, :] + decay * self.peer[:, 0:rows, :]
            self.joined[:, pl.ds(rows, 8), :] = decay * self.peer[:, rows : rows + 8, :]

            def copy(chip):
                return dict(
                    src_ref=self.joined.at[chip, pl.ds(0, self.sent)],
                    dst_ref=self.everything.at[self.z],
                )

            def to(i, carry):
                chip = far_first(self.z, i, self.chips)
                pltpu.make_async_remote_copy(
                    **copy(chip),
                    send_sem=self.send1,
                    recv_sem=self.recv1,
                    device_id={"ctx": 2 * chip},
                    device_id_type=MESH,
                ).start()
                return carry

            lax.fori_loop(0, self.chips - 1, to, 0)
            if self.near == 1:
                pltpu.make_async_copy(*copy(self.z).values(), self.recv1).start()
            else:
                pltpu.make_async_remote_copy(
                    **copy(self.z),
                    send_sem=self.send1,
                    recv_sem=self.recv1,
                    device_id={"ctx": 2 * self.z},
                    device_id_type=MESH,
                ).start()

    def work(self):
        count, rows = self.chips, self.rows

        @pl.when(self.core == 0)
        def _():
            wait_bytes(self.everything, self.recv1)
            before = jnp.zeros((rows, LANES), F32)
            for k in range(count):
                at = count - 1 - k if self.near == 1 else k
                self.found[at] = before.astype(BF16)
                decay = jnp.broadcast_to(self.decays[at, rows : rows + 1, :], (rows, LANES))
                before = decay * before + self.everything[at, 0:rows, :]

            def copy(chip):
                return pltpu.make_async_remote_copy(
                    src_ref=self.found.at[chip],
                    dst_ref=self.into.at[self.z],
                    send_sem=self.send2,
                    recv_sem=self.recv2,
                    device_id={"ctx": 2 * chip + self.near},
                    device_id_type=MESH,
                )

            def to(i, carry):
                copy(far_first(self.z, i, count)).start()
                return carry

            lax.fori_loop(0, count - 1, to, 0)
            if self.near == 1:
                copy(self.z).start()
            else:
                pltpu.make_async_copy(self.found.at[self.z], self.into.at[self.z], self.recv2).start()

    def result(self):
        @pl.when(self.core == self.near)
        def _():
            wait_bytes(self.into, self.recv2)
            pltpu.make_async_remote_copy(
                src_ref=self.into,
                dst_ref=self.into,
                send_sem=self.send3,
                recv_sem=self.recv3,
                device_id={"ctx": 2 * self.z + 1 - self.near},
                device_id_type=MESH,
            ).start()

        @pl.when(self.core != self.near)
        def _():
            wait_bytes(self.into, self.recv3)

        halves = []
        for half in range(2):
            at = pl.ds(half * self.chips // 2, self.chips // 2)
            peer = self.peer[at]
            decay = peer[:, self.rows : self.rows + 1, :]
            part = decay * self.into[at].astype(F32) + peer[:, 0 : self.rows, :]
            halves.append(part.reshape(LANES, LANES))
        return split(jnp.concatenate(halves, axis=1))

    def finish(self):
        @pl.when(self.core == self.near)
        def _():
            wait_bytes(self.start, self.peer_send)
            wait_bytes(self.into, self.send3)

        @pl.when(self.core != self.near)
        def _():
            wait_bytes(self.joined.at[pl.ds(0, self.chips - self.near), pl.ds(0, self.sent)], self.send1)

        @pl.when(self.core == 0)
        def _():
            wait_bytes(self.found.at[pl.ds(0, self.chips - 1 + self.near)], self.send2)


class Total:
    def __init__(self, peers, tp, part, taken, share, full, sems):
        self.peers, self.tp = peers, tp
        self.part, self.taken, self.share, self.full = part, taken, share, full
        self.send1, self.recv1, self.send2, self.recv2 = [sems.at[i] for i in range(4)]

    def send(self, value):
        self.part[...] = value.reshape(self.part.shape)

        def to(i, carry):
            there = far_first(self.tp, i, self.peers)
            pltpu.make_async_remote_copy(
                src_ref=self.part.at[there],
                dst_ref=self.taken.at[self.tp],
                send_sem=self.send1,
                recv_sem=self.recv1,
                device_id={"tp": there},
                device_id_type=MESH,
            ).start()
            return carry

        lax.fori_loop(0, self.peers - 1, to, 0)
        pltpu.make_async_copy(self.part.at[self.tp], self.taken.at[self.tp], self.recv1).start()

    def add(self):
        wait_bytes(self.taken, self.recv1)
        total = self.taken[0]
        for k in range(1, self.peers):
            total = total + self.taken[k]
        self.share[...] = total

        def to(i, carry):
            there = far_first(self.tp, i, self.peers)
            pltpu.make_async_remote_copy(
                src_ref=self.share,
                dst_ref=self.full.at[self.tp],
                send_sem=self.send2,
                recv_sem=self.recv2,
                device_id={"tp": there},
                device_id_type=MESH,
            ).start()
            return carry

        lax.fori_loop(0, self.peers - 1, to, 0)
        pltpu.make_async_copy(self.share, self.full.at[self.tp], self.recv2).start()

    def result(self):
        wait_bytes(self.full, self.recv2)
        return self.full[...].reshape(LANES, LANES)

    def finish(self):
        wait_bytes(self.part.at[pl.ds(0, self.peers - 1)], self.send1)
        wait_bytes(self.full.at[pl.ds(0, self.peers - 1)], self.send2)


class Columns:
    def __init__(self, chips, peers, z, core, tp, inputs, stage, cols, sems):
        self.chips, self.peers = chips, peers
        self.z, self.core, self.tp = z, core, tp
        self.inputs, self.stage, self.cols = inputs, stage, cols
        self.send1, self.recv1, self.send2, self.recv2, self.send3, self.recv3 = [
            sems.at[i] for i in range(6)
        ]
        self.share = 2 * LANES // peers
        self.sender = lax.div(tp * self.share, LANES)
        self.row = pl.multiple_of(lax.rem(tp * self.share, LANES), self.share)

    def send(self):
        @pl.when(self.core == self.sender)
        def _():
            def block(chip):
                at = pl.multiple_of(chip * 2 * LANES, 2 * LANES)
                return self.inputs.at[pl.ds(self.row, self.share), pl.ds(at, 2 * LANES)]

            def to(i, carry):
                chip = far_first(self.z, i, self.chips)
                pltpu.make_async_remote_copy(
                    src_ref=block(chip),
                    dst_ref=self.stage.at[self.z],
                    send_sem=self.send1,
                    recv_sem=self.recv1,
                    device_id={"ctx": 2 * chip + self.core},
                    device_id_type=MESH,
                ).start()
                return carry

            lax.fori_loop(0, self.chips - 1, to, 0)
            pltpu.make_async_copy(block(self.z), self.stage.at[self.z], self.recv1).start()

    def share_out(self):
        @pl.when(self.core == self.sender)
        def _():
            wait_bytes(self.stage, self.recv1)

            def half(core):
                at = pl.multiple_of(core * LANES, LANES)
                return self.stage.at[:, :, pl.ds(at, LANES)]

            pltpu.make_async_remote_copy(
                src_ref=half(1 - self.core),
                dst_ref=self.cols.at[:, self.tp],
                send_sem=self.send2,
                recv_sem=self.recv2,
                device_id={"ctx": 2 * self.z + 1 - self.core},
                device_id_type=MESH,
            ).start()
            pltpu.make_async_copy(half(self.core), self.cols.at[:, self.tp], self.recv2).start()

    def spread(self):
        mine = self.cols.at[:, self.tp]
        wait_bytes(mine, self.recv2)

        def to(i, carry):
            there = far_first(self.tp, i, self.peers)
            pltpu.make_async_remote_copy(
                src_ref=mine,
                dst_ref=mine,
                send_sem=self.send3,
                recv_sem=self.recv3,
                device_id={"tp": there},
                device_id_type=MESH,
            ).start()
            return carry

        lax.fori_loop(0, self.peers - 1, to, 0)

    def arrived(self):
        wait_bytes(self.cols.at[:, pl.ds(0, self.peers - 1)], self.recv3)

    def finish(self):
        @pl.when(self.core == self.sender)
        def _():
            sent = self.inputs.at[pl.ds(0, self.share), pl.ds(0, (self.chips - 1) * 2 * LANES)]
            wait_bytes(sent, self.send1)
            wait_bytes(self.cols.at[:, self.tp], self.send2)

        wait_bytes(self.cols.at[:, pl.ds(0, self.peers - 1)], self.send3)


def kernel(
    chips, peers,
    inputs_hbm, w_hbm, b_hbm, c_hbm, ld_hbm, skip, dout_hbm,
    dw_ref, db_ref, dc_ref,
    inputs, b_ref, c_ref, ld_ref, dout_ref,
    gw, gg, stage, cols,
    a_start, a_peer, a_joined, a_all, a_found, a_into,
    s_start, s_peer, s_joined, s_all, s_found, s_into,
    b_part, b_taken, b_share, b_full,
    c_part, c_taken, c_share, c_full,
    ring_send, ring_recv, sib_recv, carry_sems, total_sems, cols_sems, fetch_sems, wave_sems,
):
    ctx, tp = lax.axis_index("ctx"), lax.axis_index("tp")
    devices = 2 * chips
    z, core = lax.div(ctx, 2), lax.rem(ctx, 2)
    heads = 4

    fetches = [
        pltpu.make_async_copy(there, here, fetch_sems.at[i])
        for i, (there, here) in enumerate(
            [
                (ld_hbm, ld_ref),
                (c_hbm, c_ref),
                (dout_hbm, dout_ref),
                (b_hbm, b_ref),
                (w_hbm, gw.at[ctx]),
                (inputs_hbm, inputs),
            ]
        )
    ]
    for fetch in fetches:
        fetch.start()

    barrier = pltpu.get_barrier_semaphore()

    near_chips = [k % chips for k in (1, -1, 2, -2)]
    side = 4 if peers == 16 else 1
    rest = peers // side
    row, place = lax.div(tp, rest), lax.rem(tp, rest)
    in_row = [row * rest + lax.rem(place + k, rest) for k in range(1, rest)]
    in_column = [lax.rem(row + k, side) * rest + place for k in range(1, side)]
    near = [{"ctx": 2 * lax.rem(z + k, chips) + c} for k in near_chips for c in range(2)]
    near += [{"ctx": 2 * z + 1 - core}] + [{"tp": t} for t in in_row + in_column]

    def greet(sem, who):
        for device in who:
            pl.semaphore_signal(sem, inc=1, device_id=device, device_id_type=MESH)
        return len(who)

    greeted = greet(barrier, near)

    ring_w = Ring(
        chips, 2, z, core, gw, ring_send.at[0], ring_send.at[1], ring_recv.at[0], sib_recv.at[0]
    )
    ring_g = Ring(
        chips, 2, z, core, gg, ring_send.at[2], ring_send.at[3], ring_recv.at[1], sib_recv.at[1]
    )
    adjoint = Carry(
        chips, z, core, 1, None, (a_start, a_peer, a_joined, a_all, a_found, a_into), carry_sems.at[0]
    )
    state = Carry(
        chips, z, core, 0, a_all, (s_start, s_peer, s_joined, s_all, s_found, s_into), carry_sems.at[1]
    )
    total_b = Total(peers, tp, b_part, b_taken, b_share, b_full, total_sems.at[0])
    columns = Columns(chips, peers, z, core, tp, inputs, stage, cols, cols_sems)
    total_c = Total(peers, tp, c_part, c_taken, c_share, c_full, total_sems.at[1])

    rows = lax.broadcasted_iota(jnp.int32, (LANES, LANES), 0)
    lanes = lax.broadcasted_iota(jnp.int32, (LANES, LANES), 1)
    upper = (rows <= lanes).astype(F32)
    first, first_rows = lanes < LANES // 2, rows < LANES // 2
    for fetch in fetches[:4]:
        fetch.wait()
    cumulative_t = []
    for q in range(2):
        pair = [jnp.broadcast_to(ld_ref[2 * q + i : 2 * q + i + 1, :], (LANES, LANES)) for i in range(2)]
        cumulative_t.append(dot(jnp.where(first_rows, pair[0], pair[1]), upper, precision=HIGHEST))
    cumulative = jnp.concatenate([part.T for part in cumulative_t], axis=1)
    block_log = cumulative[LANES - 1 : LANES, :]
    block_decay = jnp.exp(block_log)
    to_end = jnp.exp(block_log - cumulative)
    from_start = jnp.exp(cumulative)
    b, c, dout = b_ref[...], c_ref[...], dout_ref[...]
    b_t = b.astype(F32).T.astype(BF16)
    c_t = c.astype(F32).T.astype(BF16)
    dout_wide = dout.astype(F32)
    started = split(from_start * dout_wide)
    adjoint.put(dot_split(c_t, started), block_decay)

    fetches[4].wait()
    pl.semaphore_wait(barrier, greeted)

    ring_w.begin()
    adjoint.hand()

    met_row = greet(wave_sems.at[0], [{"tp": t} for t in in_row])
    reach = 2
    while 2 * reach <= chips // 2:
        at = wave_sems.at[1 if reach == 2 else 2]
        met = greet(at, [{"ctx": 2 * lax.rem(z + k, chips) + core} for k in (reach, chips - reach)])
        pl.semaphore_wait(at, met)
        reach *= 2
    pl.semaphore_wait(wave_sems.at[0], met_row)
    fetches[5].wait()

    ring_w.step(2)
    ring_w.step(1)
    adjoint.send()

    def project(total, chip):
        at = pl.multiple_of(chip * 2 * LANES, 2 * LANES)
        block = gw[pl.ds(2 * chip, 2)].reshape(2 * LANES, -1)
        return total + dot(inputs[:, pl.ds(at, 2 * LANES)], block)

    ring_w.step(4)
    ring_w.step(3)
    columns.send()
    ring_w.arrived(0)
    projected = project(jnp.zeros((LANES, 2 * LANES), F32), z)
    for k in (1, 2):
        projected = project(projected, ring_w.source(k))
        ring_w.arrived(k)
        projected = project(projected, ring_w.sibling_source(k))
    ring_w.step(6)
    ring_w.step(5)
    adjoint.work()

    scores_t = dot(b, c, SECOND_T)
    later = lanes >= rows
    within, within_t = [], []
    for h in range(heads):
        q, side = h // 2, (h % 2) * (LANES // 2)
        column = cumulative[:, q * LANES + side : q * LANES + side + 1]
        row = cumulative_t[q][side : side + 1, :]
        within.append(jnp.where(rows >= lanes, jnp.exp(jnp.where(rows >= lanes, column - row, 0.0)), 0.0))
        within_t.append(jnp.where(later, jnp.exp(jnp.where(later, row - column, 0.0)), 0.0))
    local = []
    for q in range(2):
        pair = dout[:, q * LANES : (q + 1) * LANES]
        sides = [dot((within_t[2 * q + i] * scores_t).astype(BF16), pair) for i in range(2)]
        scale = jnp.where(first, skip[2 * q], skip[2 * q + 1])
        local.append(jnp.where(first, sides[0], sides[1]) + scale * pair.astype(F32))
    local = jnp.concatenate(local, axis=1)

    columns.share_out()
    for k in range(3, chips // 2 - 1):
        projected = project(projected, ring_w.source(k))
        ring_w.arrived(k)
        projected = project(projected, ring_w.sibling_source(k))
    ring_w.step(8)
    ring_w.step(7)

    k = chips // 2 - 1
    projected = project(projected, ring_w.source(k))
    ring_w.arrived(k)
    projected = project(projected, ring_w.sibling_source(k))
    ring_w.arrived(chips // 2)
    projected = project(projected, ring_w.source(chips // 2))
    values = projected.astype(BF16)
    ended = split(to_end * values.astype(F32))
    state.put(dot_split(b_t, ended), block_decay)
    state.hand()
    columns.spread()
    state.send()
    adjoint_in = adjoint.result()
    grad_values = local + to_end * dot_split(b, adjoint_in)
    gg[ctx] = grad_values.astype(BF16)
    ring_g.begin()

    d_b = carried(ended, adjoint_in)
    d_c = jnp.zeros((LANES, LANES), F32)
    for h in range(heads):
        q = h // 2
        mine = first if h % 2 == 0 else jnp.logical_not(first)
        part = values[:, q * LANES : (q + 1) * LANES]
        part = jnp.where(mine, part.astype(F32), 0.0).astype(BF16)
        pair = dout[:, q * LANES : (q + 1) * LANES]
        weights = (within[h] * dot(pair, part, SECOND_T)).astype(BF16)
        weights_t = (within_t[h] * dot(part, pair, SECOND_T)).astype(BF16)
        d_c = d_c + dot(weights, b)
        d_b = d_b + dot(weights_t, c)
    total_b.send(d_b)
    ring_g.step(2)
    ring_g.step(1)

    def project_back(total, chip):
        return total + dot(
            cols[chip].reshape(2 * LANES, LANES).astype(F32).T.astype(BF16),
            gg[pl.ds(2 * chip, 2)].reshape(2 * LANES, -1),
        )

    columns.arrived()
    ring_g.arrived(0)
    grad_w = project_back(jnp.zeros((LANES, 2 * LANES), F32), z)
    ring_g.step(4)
    ring_g.step(3)
    state.work()
    total_b.add()

    def back_both(total, k):
        total = project_back(total, ring_g.source(k))
        ring_g.arrived(k)
        return project_back(total, ring_g.sibling_source(k))

    for k in (1, 2):
        grad_w = back_both(grad_w, k)
    ring_g.step(6)
    ring_g.step(5)
    state_in = state.result()
    d_c = d_c + carried(started, state_in)
    total_c.send(d_c)
    for k in range(3, chips // 2 - 1):
        grad_w = back_both(grad_w, k)
    ring_g.step(8)
    ring_g.step(7)
    total_c.add()
    grad_w = back_both(grad_w, chips // 2 - 1)
    ring_g.arrived(chips // 2)
    dw_ref[...] = project_back(grad_w, ring_g.source(chips // 2))
    db_ref[...] = total_b.result()
    dc_ref[...] = total_c.result()

    ring_w.finish()
    ring_g.finish()
    adjoint.finish()
    state.finish()
    total_b.finish()
    total_c.finish()
    columns.finish()


def solution(mesh):
    devices, peers = mesh.shape["ctx"], mesh.shape["tp"]
    chips = devices // 2

    def per_device(inputs, w_in, b_in, c_in, log_decay, skip, d_out):
        tokens, width = d_out.shape
        rows = LANES // (chips // 2)
        vmem, hbm = pl.BlockSpec(memory_space=pltpu.VMEM), pl.BlockSpec(memory_space=pltpu.HBM)
        def carry_scratch(sent):
            return [
                pltpu.VMEM((chips, rows + 8, LANES), F32),
                pltpu.VMEM((chips, rows + 8, LANES), F32),
                pltpu.VMEM((chips, rows + 8, LANES), F32),
                pltpu.VMEM((chips, sent, LANES), F32),
                pltpu.VMEM((chips, rows, LANES), BF16),
                pltpu.VMEM((chips, rows, LANES), BF16),
            ]

        total_scratch = [
            pltpu.VMEM((peers, tokens // peers, LANES), F32),
            pltpu.VMEM((peers, tokens // peers, LANES), F32),
            pltpu.VMEM((tokens // peers, LANES), F32),
            pltpu.VMEM((peers, tokens // peers, LANES), F32),
        ]
        half = chips // 2
        return pl.pallas_call(
            functools.partial(kernel, chips, peers),
            out_shape=(
                jax.ShapeDtypeStruct(w_in.shape, F32),
                jax.ShapeDtypeStruct(b_in.shape, F32),
                jax.ShapeDtypeStruct(c_in.shape, F32),
            ),
            in_specs=[hbm] * 5 + [pl.BlockSpec(memory_space=pltpu.SMEM), hbm],
            out_specs=(vmem, vmem, vmem),
            scratch_shapes=[
                pltpu.VMEM(inputs.shape, BF16),
                pltpu.VMEM(b_in.shape, BF16),
                pltpu.VMEM(c_in.shape, BF16),
                pltpu.VMEM(log_decay.shape[::-1], F32),
                pltpu.VMEM(d_out.shape, BF16),
                pltpu.VMEM((devices, tokens, width), BF16),
                pltpu.VMEM((devices, tokens, width), BF16),
                pltpu.VMEM((chips, 2 * tokens // peers, 2 * LANES), BF16),
                pltpu.VMEM((chips, peers, 2 * tokens // peers, LANES), BF16),
            ]
            + carry_scratch(rows + 8)
            + carry_scratch(rows)
            + total_scratch * 2
            + [
                pltpu.SemaphoreType.DMA((4,)),
                pltpu.SemaphoreType.DMA((2, half + 1, 2)),
                pltpu.SemaphoreType.DMA((2, half + 1, 2)),
                pltpu.SemaphoreType.DMA((2, 8)),
                pltpu.SemaphoreType.DMA((2, 4)),
                pltpu.SemaphoreType.DMA((6,)),
                pltpu.SemaphoreType.DMA((6,)),
                pltpu.SemaphoreType.REGULAR((3,)),
            ],
            compiler_params=pltpu.CompilerParams(
                collective_id=0, has_side_effects=True, vmem_limit_bytes=60 * 1024 * 1024
            ),
        )(inputs, w_in, b_in, c_in, log_decay.T, skip, d_out)

    return jax.shard_map(
        per_device,
        mesh=mesh,
        in_specs=(
            P("ctx", None),
            P("ctx", "tp"),
            P("ctx", None),
            P("ctx", None),
            P("ctx", "tp"),
            P("tp"),
            P("ctx", "tp"),
        ),
        out_specs=(P("ctx", "tp"), P("ctx", None), P("ctx", None)),
        check_vma=False,
    )
```

```python
import functools

import jax
import jax.numpy as jnp
from jax import lax
from jax.experimental import pallas as pl
from jax.experimental.pallas import tpu as pltpu
from jax.sharding import PartitionSpec as P

F32 = jnp.float32
BF16 = jnp.bfloat16
MESH = pl.DeviceIdType.MESH
HIGHEST = lax.Precision.HIGHEST
LANES = 128
RING_W, RING_G = ((2,), 2), ((2,), 2)
PLAIN = ((1,), (0,))
SECOND_T = ((1,), (1,))


def dot(a, b, dims=PLAIN, precision=None):
    return lax.dot_general(a, b, (dims, ((), ())), precision=precision, preferred_element_type=F32)


def split(x):
    high = x.astype(BF16)
    return high, (x - high.astype(F32)).astype(BF16)


def dot_split(a, b_pair):
    return dot(a, b_pair[0]) + dot(a, b_pair[1])


def carried(a_pair, b_pair):
    return sum(dot(a_pair[i], b_pair[j], SECOND_T) for i, j in ((0, 0), (0, 1), (1, 0)))


def wait_bytes(ref, sem):
    pltpu.make_async_copy(ref, ref, sem).wait()


def far_first(place, i, count):
    aside = lax.div(i + 1, 2)
    return lax.rem(place + count // 2 + jnp.where(lax.rem(i, 2) == 1, count - aside, aside), count)


class Ring:
    def __init__(self, chips, legs, parts, z, core, blocks, ring_send, sib_send, ring_recv, sib_recv):
        self.chips, self.parts, self.half = chips, parts, chips // 2
        self.leg, self.order, at = {}, [], 0
        while at < self.half:
            self.leg[at] = min(legs[len(self.leg) % len(legs)], self.half - at)
            self.order += range(at + self.leg[at], at, -1)
            at += self.leg[at]
        self.z, self.core, self.blocks = z, core, blocks
        self.ring_send, self.sib_send = ring_send, sib_send
        self.ring_recv, self.sib_recv = ring_recv, sib_recv
        self.sibling, self.mine = 2 * z + 1 - core, 2 * z + core
        self.rows = blocks.shape[1] // parts

    def copy(self, ref, to, send, recv):
        pltpu.make_async_remote_copy(
            src_ref=ref, dst_ref=ref, send_sem=send, recv_sem=recv, device_id={"ctx": to}, device_id_type=MESH
        ).start()

    def part(self, block, p):
        return self.blocks.at[block, pl.ds(p * self.rows, self.rows)]

    def back(self, k):
        return lax.rem(self.z + (self.chips - k), self.chips)

    def ahead(self, k):
        return lax.rem(self.z + k, self.chips)

    def source(self, k):
        return jnp.where(self.core == 0, self.back(k), self.ahead(k))

    def sibling_source(self, k):
        return jnp.where(self.core == 0, self.ahead(k), self.back(k))

    def onward(self, k):
        return 2 * self.sibling_source(k) + self.core

    def begin(self):
        leg = self.leg[0]
        for p in range(self.parts):
            recv = self.ring_recv.at[leg, self.core * self.parts + p]
            self.copy(self.part(self.mine, p), 2 * self.ahead(leg), self.ring_send, recv)
            self.copy(self.part(self.mine, p), 2 * self.back(leg) + 1, self.ring_send, recv)
        for s in range(leg - 1, 0, -1):
            recv = self.ring_recv.at[s, 0]
            self.copy(self.blocks.at[self.mine], 2 * self.ahead(s), self.ring_send, recv)
            self.copy(self.blocks.at[self.mine], 2 * self.back(s) + 1, self.ring_send, recv)
        self.copy(self.blocks.at[self.mine], self.sibling, self.sib_send, self.sib_recv.at[0])

    def step(self, k):
        base = 2 * self.source(k)
        whole = self.blocks.at[base + self.core if k == self.half else pl.ds(base, 2)]
        if k == self.half:
            for p in range(self.parts):
                wait_bytes(self.part(base + self.core, p), self.ring_recv.at[k, p])
        elif k not in self.leg:
            wait_bytes(whole, self.ring_recv.at[k, 0])
        else:
            leg = self.leg[k]
            there = k + leg
            for p in range(self.parts):
                for h in range(2):
                    at = h * self.parts + p
                    wait_bytes(self.part(base + h, p), self.ring_recv.at[k, at])
                    if there < self.half:
                        recv = self.ring_recv.at[there, at]
                        self.copy(self.part(base + h, p), self.onward(leg), self.ring_send, recv)
                if there == self.half:
                    recv = self.ring_recv.at[there, p]
                    self.copy(self.part(base + self.core, p), self.onward(leg), self.ring_send, recv)
            for s in range(leg - 1, 0, -1):
                self.copy(whole, self.onward(s), self.ring_send, self.ring_recv.at[k + s, 0])
        self.copy(whole, self.sibling, self.sib_send, self.sib_recv.at[k])

    def steps(self, *ks):
        for k in sorted((k for k in ks if k <= self.half), key=self.order.index):
            self.step(k)

    def arrived(self, k):
        got = self.blocks.at[pl.ds(0, 1 if k == 0 or k == self.half else 2)]
        wait_bytes(got, self.sib_recv.at[k])

    def finish(self):
        wait_bytes(self.blocks.at[pl.ds(0, self.chips - 1)], self.ring_send)
        wait_bytes(self.blocks.at[pl.ds(0, self.chips)], self.sib_send)


class Carry:
    def __init__(self, chips, z, core, near, decays, refs, sems):
        self.chips, self.z, self.core, self.near = chips, z, core, near
        self.start, self.peer, self.joined, self.everything, self.found, self.into = refs
        self.peer_send, self.peer_recv, self.send1, self.recv1, self.send2, self.recv2, self.send3, self.recv3 = [
            sems.at[i] for i in range(8)
        ]
        self.rows = self.into.shape[1]
        self.decays = self.everything if decays is None else decays
        self.sent = self.rows + (decays is None)

    def put(self, state, decay):
        slices, rows = self.chips, self.rows
        for half in range(2):
            at = pl.ds(half * slices // 2, slices // 2)
            part = state[:, half * LANES : (half + 1) * LANES]
            self.start[at, pl.ds(0, rows), :] = part.reshape(slices // 2, rows, LANES)
            wide = jnp.broadcast_to(decay[:, half * LANES : (half + 1) * LANES], (8, LANES))
            self.start[at, pl.ds(rows, 8), :] = jnp.broadcast_to(wide[None], (slices // 2, 8, LANES))

    def hand(self):
        @pl.when(self.core == self.near)
        def _():
            pltpu.make_async_remote_copy(
                src_ref=self.start,
                dst_ref=self.peer,
                send_sem=self.peer_send,
                recv_sem=self.peer_recv,
                device_id={"ctx": 2 * self.z + 1 - self.near},
                device_id_type=MESH,
            ).start()
            self.peer[:, pl.ds(0, self.rows), :] = jnp.zeros((self.chips, self.rows, LANES), F32)
            self.peer[:, pl.ds(self.rows, 8), :] = jnp.ones((self.chips, 8, LANES), F32)

    def send(self):
        rows = self.rows

        @pl.when(self.core != self.near)
        def _():
            wait_bytes(self.peer, self.peer_recv)
            decay = self.start[:, rows : rows + 1, :]
            self.joined[:, pl.ds(0, rows), :] = self.start[:, 0:rows, :] + decay * self.peer[:, 0:rows, :]
            self.joined[:, pl.ds(rows, 8), :] = decay * self.peer[:, rows : rows + 8, :]

            def copy(chip):
                return dict(
                    src_ref=self.joined.at[chip, pl.ds(0, self.sent)],
                    dst_ref=self.everything.at[self.z, pl.ds(0, self.sent)],
                )

            def to(i, carry):
                chip = far_first(self.z, i, self.chips)
                pltpu.make_async_remote_copy(
                    **copy(chip),
                    send_sem=self.send1,
                    recv_sem=self.recv1,
                    device_id={"ctx": 2 * chip},
                    device_id_type=MESH,
                ).start()
                return carry

            lax.fori_loop(0, self.chips - 1, to, 0)
            if self.near == 1:
                pltpu.make_async_copy(*copy(self.z).values(), self.recv1).start()
            else:
                pltpu.make_async_remote_copy(
                    **copy(self.z),
                    send_sem=self.send1,
                    recv_sem=self.recv1,
                    device_id={"ctx": 2 * self.z},
                    device_id_type=MESH,
                ).start()

    def work(self):
        count, rows = self.chips, self.rows

        @pl.when(self.core == 0)
        def _():
            wait_bytes(self.everything.at[:, pl.ds(0, self.sent)], self.recv1)
            before = jnp.zeros((rows, LANES), F32)
            for k in range(count):
                at = count - 1 - k if self.near == 1 else k
                self.found[at] = before.astype(BF16)
                decay = jnp.broadcast_to(self.decays[at, rows : rows + 1, :], (rows, LANES))
                before = decay * before + self.everything[at, 0:rows, :]

            def copy(chip):
                return pltpu.make_async_remote_copy(
                    src_ref=self.found.at[chip],
                    dst_ref=self.into.at[self.z],
                    send_sem=self.send2,
                    recv_sem=self.recv2,
                    device_id={"ctx": 2 * chip + self.near},
                    device_id_type=MESH,
                )

            def to(i, carry):
                copy(far_first(self.z, i, count)).start()
                return carry

            lax.fori_loop(0, count - 1, to, 0)
            if self.near == 1:
                copy(self.z).start()
            else:
                pltpu.make_async_copy(self.found.at[self.z], self.into.at[self.z], self.recv2).start()

    def result(self):
        @pl.when(self.core == self.near)
        def _():
            wait_bytes(self.into, self.recv2)
            pltpu.make_async_remote_copy(
                src_ref=self.into,
                dst_ref=self.into,
                send_sem=self.send3,
                recv_sem=self.recv3,
                device_id={"ctx": 2 * self.z + 1 - self.near},
                device_id_type=MESH,
            ).start()

        @pl.when(self.core != self.near)
        def _():
            wait_bytes(self.into, self.recv3)

        halves = []
        for half in range(2):
            at = pl.ds(half * self.chips // 2, self.chips // 2)
            peer = self.peer[at]
            decay = peer[:, self.rows : self.rows + 1, :]
            part = decay * self.into[at].astype(F32) + peer[:, 0 : self.rows, :]
            halves.append(part.reshape(LANES, LANES))
        return split(jnp.concatenate(halves, axis=1))

    def finish(self):
        @pl.when(self.core == self.near)
        def _():
            wait_bytes(self.start, self.peer_send)
            wait_bytes(self.into, self.send3)

        @pl.when(self.core != self.near)
        def _():
            wait_bytes(self.joined.at[pl.ds(0, self.chips - self.near), pl.ds(0, self.sent)], self.send1)

        @pl.when(self.core == 0)
        def _():
            wait_bytes(self.found.at[pl.ds(0, self.chips - 1 + self.near)], self.send2)


class Total:
    def __init__(self, peers, tp, part, taken, share, full, sems):
        self.peers, self.tp = peers, tp
        self.part, self.taken, self.share, self.full = part, taken, share, full
        self.send1, self.recv1, self.send2, self.recv2 = [sems.at[i] for i in range(4)]

    def send(self, value):
        self.part[...] = value.reshape(self.part.shape)

        def to(i, carry):
            there = far_first(self.tp, i, self.peers)
            pltpu.make_async_remote_copy(
                src_ref=self.part.at[there],
                dst_ref=self.taken.at[self.tp],
                send_sem=self.send1,
                recv_sem=self.recv1,
                device_id={"tp": there},
                device_id_type=MESH,
            ).start()
            return carry

        lax.fori_loop(0, self.peers - 1, to, 0)
        pltpu.make_async_copy(self.part.at[self.tp], self.taken.at[self.tp], self.recv1).start()

    def add(self):
        wait_bytes(self.taken, self.recv1)
        total = self.taken[0]
        for k in range(1, self.peers):
            total = total + self.taken[k]
        self.share[...] = total

        def to(i, carry):
            there = far_first(self.tp, i, self.peers)
            pltpu.make_async_remote_copy(
                src_ref=self.share,
                dst_ref=self.full.at[self.tp],
                send_sem=self.send2,
                recv_sem=self.recv2,
                device_id={"tp": there},
                device_id_type=MESH,
            ).start()
            return carry

        lax.fori_loop(0, self.peers - 1, to, 0)
        pltpu.make_async_copy(self.share, self.full.at[self.tp], self.recv2).start()

    def result(self):
        wait_bytes(self.full, self.recv2)
        return self.full[...].reshape(LANES, LANES)

    def finish(self):
        wait_bytes(self.part.at[pl.ds(0, self.peers - 1)], self.send1)
        wait_bytes(self.full.at[pl.ds(0, self.peers - 1)], self.send2)


class Columns:
    def __init__(self, chips, peers, z, core, tp, inputs, stage, cols, sems):
        self.chips, self.peers = chips, peers
        self.z, self.core, self.tp = z, core, tp
        self.inputs, self.stage, self.cols = inputs, stage, cols
        self.send1, self.recv1, self.send2, self.recv2, self.send3, self.recv3 = [
            sems.at[i] for i in range(6)
        ]
        self.share = 2 * LANES // peers
        self.sender = lax.div(tp * self.share, LANES)
        self.row = pl.multiple_of(lax.rem(tp * self.share, LANES), self.share)

    def send(self):
        @pl.when(self.core == self.sender)
        def _():
            def block(chip):
                at = pl.multiple_of(chip * 2 * LANES, 2 * LANES)
                return self.inputs.at[pl.ds(self.row, self.share), pl.ds(at, 2 * LANES)]

            def to(i, carry):
                chip = far_first(self.z, i, self.chips)
                pltpu.make_async_remote_copy(
                    src_ref=block(chip),
                    dst_ref=self.stage.at[self.z],
                    send_sem=self.send1,
                    recv_sem=self.recv1,
                    device_id={"ctx": 2 * chip + self.core},
                    device_id_type=MESH,
                ).start()
                return carry

            lax.fori_loop(0, self.chips - 1, to, 0)
            pltpu.make_async_copy(block(self.z), self.stage.at[self.z], self.recv1).start()

    def share_out(self):
        @pl.when(self.core == self.sender)
        def _():
            wait_bytes(self.stage, self.recv1)

            def half(core):
                at = pl.multiple_of(core * LANES, LANES)
                return self.stage.at[:, :, pl.ds(at, LANES)]

            pltpu.make_async_remote_copy(
                src_ref=half(1 - self.core),
                dst_ref=self.cols.at[:, self.tp],
                send_sem=self.send2,
                recv_sem=self.recv2,
                device_id={"ctx": 2 * self.z + 1 - self.core},
                device_id_type=MESH,
            ).start()
            pltpu.make_async_copy(half(self.core), self.cols.at[:, self.tp], self.recv2).start()

    def spread(self):
        mine = self.cols.at[:, self.tp]
        wait_bytes(mine, self.recv2)

        def to(i, carry):
            there = far_first(self.tp, i, self.peers)
            pltpu.make_async_remote_copy(
                src_ref=mine,
                dst_ref=mine,
                send_sem=self.send3,
                recv_sem=self.recv3,
                device_id={"tp": there},
                device_id_type=MESH,
            ).start()
            return carry

        lax.fori_loop(0, self.peers - 1, to, 0)

    def arrived(self):
        wait_bytes(self.cols.at[:, pl.ds(0, self.peers - 1)], self.recv3)

    def finish(self):
        @pl.when(self.core == self.sender)
        def _():
            sent = self.inputs.at[pl.ds(0, self.share), pl.ds(0, (self.chips - 1) * 2 * LANES)]
            wait_bytes(sent, self.send1)
            wait_bytes(self.cols.at[:, self.tp], self.send2)

        wait_bytes(self.cols.at[:, pl.ds(0, self.peers - 1)], self.send3)


def kernel(
    chips, peers,
    inputs_hbm, w_hbm, b_hbm, c_hbm, ld_hbm, skip, dout_hbm,
    dw_ref, db_ref, dc_ref,
    inputs, b_ref, c_ref, ld_ref, dout_ref,
    gw, gg, stage, cols,
    a_start, a_peer, a_joined, a_all, a_found, a_into,
    s_start, s_peer, s_joined, s_all, s_found, s_into,
    b_part, b_taken, b_share, b_full,
    c_part, c_taken, c_share, c_full,
    ring_send, ring_recv, sib_recv, carry_sems, total_sems, cols_sems, fetch_sems, wave_sems,
):
    ctx, tp = lax.axis_index("ctx"), lax.axis_index("tp")
    devices = 2 * chips
    z, core = lax.div(ctx, 2), lax.rem(ctx, 2)
    heads = 4

    fetches = [
        pltpu.make_async_copy(there, here, fetch_sems.at[i])
        for i, (there, here) in enumerate(
            [
                (ld_hbm, ld_ref),
                (c_hbm, c_ref),
                (dout_hbm, dout_ref),
                (b_hbm, b_ref),
                (w_hbm, gw.at[ctx]),
                (inputs_hbm, inputs),
            ]
        )
    ]
    for fetch in fetches:
        fetch.start()

    barrier = pltpu.get_barrier_semaphore()

    near_chips = [k % chips for k in (1, -1, 2, -2)]
    side = 4 if peers == 16 else 1
    rest = peers // side
    row, place = lax.div(tp, rest), lax.rem(tp, rest)
    in_row = [row * rest + lax.rem(place + k, rest) for k in range(1, rest)]
    in_column = [lax.rem(row + k, side) * rest + place for k in range(1, side)]
    near = [{"ctx": 2 * lax.rem(z + k, chips) + c} for k in near_chips for c in range(2)]
    near += [{"ctx": 2 * z + 1 - core}] + [{"tp": t} for t in in_row + in_column]

    def greet(sem, who):
        for device in who:
            pl.semaphore_signal(sem, inc=1, device_id=device, device_id_type=MESH)
        return len(who)

    greeted = greet(barrier, near)

    ring_w = Ring(
        chips, *RING_W, z, core, gw, ring_send.at[0], ring_send.at[1], ring_recv.at[0], sib_recv.at[0]
    )
    ring_g = Ring(
        chips, *RING_G, z, core, gg, ring_send.at[2], ring_send.at[3], ring_recv.at[1], sib_recv.at[1]
    )
    adjoint = Carry(
        chips, z, core, 1, None, (a_start, a_peer, a_joined, a_all, a_found, a_into), carry_sems.at[0]
    )
    state = Carry(
        chips, z, core, 0, a_all, (s_start, s_peer, s_joined, s_all, s_found, s_into), carry_sems.at[1]
    )
    total_b = Total(peers, tp, b_part, b_taken, b_share, b_full, total_sems.at[0])
    columns = Columns(chips, peers, z, core, tp, inputs, stage, cols, cols_sems)
    total_c = Total(peers, tp, c_part, c_taken, c_share, c_full, total_sems.at[1])

    rows = lax.broadcasted_iota(jnp.int32, (LANES, LANES), 0)
    lanes = lax.broadcasted_iota(jnp.int32, (LANES, LANES), 1)
    upper = (rows <= lanes).astype(F32)
    first, first_rows = lanes < LANES // 2, rows < LANES // 2
    for fetch in fetches[:4]:
        fetch.wait()
    cumulative_t = []
    for q in range(2):
        pair = [jnp.broadcast_to(ld_ref[2 * q + i : 2 * q + i + 1, :], (LANES, LANES)) for i in range(2)]
        cumulative_t.append(dot(jnp.where(first_rows, pair[0], pair[1]), upper, precision=HIGHEST))
    cumulative = jnp.concatenate([part.T for part in cumulative_t], axis=1)
    block_log = cumulative[LANES - 1 : LANES, :]
    block_decay = jnp.exp(block_log)
    to_end = jnp.exp(block_log - cumulative)
    from_start = jnp.exp(cumulative)
    b, c, dout = b_ref[...], c_ref[...], dout_ref[...]
    b_t = b.astype(F32).T.astype(BF16)
    c_t = c.astype(F32).T.astype(BF16)
    dout_wide = dout.astype(F32)
    started = split(from_start * dout_wide)
    adjoint.put(dot_split(c_t, started), block_decay)

    fetches[4].wait()
    pl.semaphore_wait(barrier, greeted)

    ring_w.begin()
    adjoint.hand()

    met_row = greet(wave_sems.at[0], [{"tp": t} for t in in_row])
    reach = 2
    while 2 * reach <= chips // 2:
        at = wave_sems.at[1 if reach == 2 else 2]
        met = greet(at, [{"ctx": 2 * lax.rem(z + k, chips) + core} for k in (reach, chips - reach)])
        pl.semaphore_wait(at, met)
        reach *= 2
    pl.semaphore_wait(wave_sems.at[0], met_row)
    fetches[5].wait()

    adjoint.send()
    ring_w.steps(1, 2)
    columns.send()

    def project(total, chip):
        at = pl.multiple_of(chip * 2 * LANES, 2 * LANES)
        block = gw[pl.ds(2 * chip, 2)].reshape(2 * LANES, -1)
        return total + dot(inputs[:, pl.ds(at, 2 * LANES)], block)

    def project_both(total, k):
        total = project(total, ring_w.source(k))
        ring_w.arrived(k)
        return project(total, ring_w.sibling_source(k))

    scores_t = dot(b, c, SECOND_T)
    later = lanes >= rows
    within, within_t = [], []
    for h in range(heads):
        q, side = h // 2, (h % 2) * (LANES // 2)
        column = cumulative[:, q * LANES + side : q * LANES + side + 1]
        row = cumulative_t[q][side : side + 1, :]
        within.append(jnp.where(rows >= lanes, jnp.exp(jnp.where(rows >= lanes, column - row, 0.0)), 0.0))
        within_t.append(jnp.where(later, jnp.exp(jnp.where(later, row - column, 0.0)), 0.0))
    local = []
    for q in range(2):
        pair = dout[:, q * LANES : (q + 1) * LANES]
        sides = [dot((within_t[2 * q + i] * scores_t).astype(BF16), pair) for i in range(2)]
        scale = jnp.where(first, skip[2 * q], skip[2 * q + 1])
        local.append(jnp.where(first, sides[0], sides[1]) + scale * pair.astype(F32))
    local = jnp.concatenate(local, axis=1)

    ring_w.steps(3, 4)
    ring_w.arrived(0)
    projected = project(jnp.zeros((LANES, 2 * LANES), F32), z)
    for k in (1, 2):
        projected = project_both(projected, k)
    ring_w.steps(5, 6)
    adjoint.work()
    columns.share_out()
    for k in range(3, chips // 2 - 1):
        projected = project_both(projected, k)
    columns.spread()
    ring_w.steps(7, 8)

    projected = project_both(projected, chips // 2 - 1)
    ring_w.arrived(chips // 2)
    projected = project(projected, ring_w.source(chips // 2))
    values = projected.astype(BF16)
    ended = split(to_end * values.astype(F32))
    state.put(dot_split(b_t, ended), block_decay)
    state.hand()
    state.send()

    adjoint_in = adjoint.result()
    grad_values = local + to_end * dot_split(b, adjoint_in)
    gg[ctx] = grad_values.astype(BF16)
    ring_g.begin()

    d_b = carried(ended, adjoint_in)
    d_c = jnp.zeros((LANES, LANES), F32)
    for h in range(heads):
        q = h // 2
        mine = first if h % 2 == 0 else jnp.logical_not(first)
        part = values[:, q * LANES : (q + 1) * LANES]
        part = jnp.where(mine, part.astype(F32), 0.0).astype(BF16)
        pair = dout[:, q * LANES : (q + 1) * LANES]
        weights = (within[h] * dot(pair, part, SECOND_T)).astype(BF16)
        weights_t = (within_t[h] * dot(part, pair, SECOND_T)).astype(BF16)
        d_c = d_c + dot(weights, b)
        d_b = d_b + dot(weights_t, c)
    total_b.send(d_b)
    ring_g.steps(1, 2)
    state.work()
    ring_g.steps(3, 4)
    total_b.add()
    ring_g.steps(5, 6)
    state_in = state.result()
    d_c = d_c + carried(started, state_in)
    total_c.send(d_c)

    def project_back(total, chip):
        return total + dot(
            cols[chip].reshape(2 * LANES, LANES).astype(F32).T.astype(BF16),
            gg[pl.ds(2 * chip, 2)].reshape(2 * LANES, -1),
        )

    def back_both(total, k):
        total = project_back(total, ring_g.source(k))
        ring_g.arrived(k)
        return project_back(total, ring_g.sibling_source(k))

    columns.arrived()
    ring_g.arrived(0)
    grad_w = project_back(jnp.zeros((LANES, 2 * LANES), F32), z)
    ring_g.steps(7, 8)
    for k in range(1, chips // 2 - 1):
        grad_w = back_both(grad_w, k)
    total_c.add()
    grad_w = back_both(grad_w, chips // 2 - 1)
    ring_g.arrived(chips // 2)
    dw_ref[...] = project_back(grad_w, ring_g.source(chips // 2))
    db_ref[...] = total_b.result()
    dc_ref[...] = total_c.result()

    ring_w.finish()
    ring_g.finish()
    adjoint.finish()
    state.finish()
    total_b.finish()
    total_c.finish()
    columns.finish()


def solution(mesh):
    devices, peers = mesh.shape["ctx"], mesh.shape["tp"]
    chips = devices // 2

    def per_device(inputs, w_in, b_in, c_in, log_decay, skip, d_out):
        tokens, width = d_out.shape
        rows = LANES // (chips // 2)
        vmem, hbm = pl.BlockSpec(memory_space=pltpu.VMEM), pl.BlockSpec(memory_space=pltpu.HBM)
        def carry_scratch(sent):
            return [
                pltpu.VMEM((chips, rows + 8, LANES), F32),
                pltpu.VMEM((chips, rows + 8, LANES), F32),
                pltpu.VMEM((chips, rows + 8, LANES), F32),
                pltpu.VMEM((chips, sent, LANES), F32),
                pltpu.VMEM((chips, rows, LANES), BF16),
                pltpu.VMEM((chips, rows, LANES), BF16),
            ]

        total_scratch = [
            pltpu.VMEM((peers, tokens // peers, LANES), F32),
            pltpu.VMEM((peers, tokens // peers, LANES), F32),
            pltpu.VMEM((tokens // peers, LANES), F32),
            pltpu.VMEM((peers, tokens // peers, LANES), F32),
        ]
        half = chips // 2
        return pl.pallas_call(
            functools.partial(kernel, chips, peers),
            out_shape=(
                jax.ShapeDtypeStruct(w_in.shape, F32),
                jax.ShapeDtypeStruct(b_in.shape, F32),
                jax.ShapeDtypeStruct(c_in.shape, F32),
            ),
            in_specs=[hbm] * 5 + [pl.BlockSpec(memory_space=pltpu.SMEM), hbm],
            out_specs=(vmem, vmem, vmem),
            scratch_shapes=[
                pltpu.VMEM(inputs.shape, BF16),
                pltpu.VMEM(b_in.shape, BF16),
                pltpu.VMEM(c_in.shape, BF16),
                pltpu.VMEM(log_decay.shape[::-1], F32),
                pltpu.VMEM(d_out.shape, BF16),
                pltpu.VMEM((devices, tokens, width), BF16),
                pltpu.VMEM((devices, tokens, width), BF16),
                pltpu.VMEM((chips, 2 * tokens // peers, 2 * LANES), BF16),
                pltpu.VMEM((chips, peers, 2 * tokens // peers, LANES), BF16),
            ]
            + carry_scratch(rows + 8)
            + carry_scratch(rows)
            + total_scratch * 2
            + [
                pltpu.SemaphoreType.DMA((4,)),
                pltpu.SemaphoreType.DMA((2, half + 1, 2 * max(RING_W[1], RING_G[1]))),
                pltpu.SemaphoreType.DMA((2, half + 1)),
                pltpu.SemaphoreType.DMA((2, 8)),
                pltpu.SemaphoreType.DMA((2, 4)),
                pltpu.SemaphoreType.DMA((6,)),
                pltpu.SemaphoreType.DMA((6,)),
                pltpu.SemaphoreType.REGULAR((3,)),
            ],
            compiler_params=pltpu.CompilerParams(
                collective_id=0, has_side_effects=True, vmem_limit_bytes=60 * 1024 * 1024
            ),
        )(inputs, w_in, b_in, c_in, log_decay.T, skip, d_out)

    return jax.shard_map(
        per_device,
        mesh=mesh,
        in_specs=(
            P("ctx", None),
            P("ctx", "tp"),
            P("ctx", None),
            P("ctx", None),
            P("ctx", "tp"),
            P("tp"),
            P("ctx", "tp"),
        ),
        out_specs=(P("ctx", "tp"), P("ctx", None), P("ctx", None)),
        check_vma=False,
    )
```

```python
import functools

import jax
import jax.numpy as jnp
from jax import lax
from jax.experimental import pallas as pl
from jax.experimental.pallas import tpu as pltpu
from jax.sharding import PartitionSpec as P

F32 = jnp.float32
BF16 = jnp.bfloat16
MESH = pl.DeviceIdType.MESH
HIGHEST = lax.Precision.HIGHEST
LANES = 128
RING_W, RING_G = ((2,), 2), ((2,), 2)
PLAIN = ((1,), (0,))
SECOND_T = ((1,), (1,))


def dot(a, b, dims=PLAIN, precision=None):
    return lax.dot_general(a, b, (dims, ((), ())), precision=precision, preferred_element_type=F32)


def split(x):
    high = x.astype(BF16)
    return high, (x - high.astype(F32)).astype(BF16)


def dot_split(a, b_pair):
    return dot(a, b_pair[0]) + dot(a, b_pair[1])


def carried(a_pair, b_pair):
    return sum(dot(a_pair[i], b_pair[j], SECOND_T) for i, j in ((0, 0), (0, 1), (1, 0)))


def wait_bytes(ref, sem):
    pltpu.make_async_copy(ref, ref, sem).wait()


def far_first(place, i, count):
    aside = lax.div(i + 1, 2)
    return lax.rem(place + count // 2 + jnp.where(lax.rem(i, 2) == 1, count - aside, aside), count)


class Ring:
    def __init__(self, chips, legs, parts, z, core, blocks, ring_send, sib_send, ring_recv, sib_recv):
        self.chips, self.parts, self.half = chips, parts, chips // 2
        self.leg, self.order, at = {}, [], 0
        while at < self.half:
            self.leg[at] = min(legs[len(self.leg) % len(legs)], self.half - at)
            self.order += range(at + self.leg[at], at, -1)
            at += self.leg[at]
        self.z, self.core, self.blocks = z, core, blocks
        self.ring_send, self.sib_send = ring_send, sib_send
        self.ring_recv, self.sib_recv = ring_recv, sib_recv
        self.sibling, self.mine = 2 * z + 1 - core, 2 * z + core
        self.rows = blocks.shape[1] // parts

    def copy(self, ref, to, send, recv):
        pltpu.make_async_remote_copy(
            src_ref=ref, dst_ref=ref, send_sem=send, recv_sem=recv, device_id={"ctx": to}, device_id_type=MESH
        ).start()

    def part(self, block, p):
        return self.blocks.at[block, pl.ds(p * self.rows, self.rows)]

    def back(self, k):
        return lax.rem(self.z + (self.chips - k), self.chips)

    def ahead(self, k):
        return lax.rem(self.z + k, self.chips)

    def source(self, k):
        return jnp.where(self.core == 0, self.back(k), self.ahead(k))

    def sibling_source(self, k):
        return jnp.where(self.core == 0, self.ahead(k), self.back(k))

    def onward(self, k):
        return 2 * self.sibling_source(k) + self.core

    def begin(self):
        leg = self.leg[0]
        for p in range(self.parts):
            recv = self.ring_recv.at[leg, self.core * self.parts + p]
            self.copy(self.part(self.mine, p), 2 * self.ahead(leg), self.ring_send, recv)
            self.copy(self.part(self.mine, p), 2 * self.back(leg) + 1, self.ring_send, recv)
        for s in range(leg - 1, 0, -1):
            recv = self.ring_recv.at[s, 0]
            self.copy(self.blocks.at[self.mine], 2 * self.ahead(s), self.ring_send, recv)
            self.copy(self.blocks.at[self.mine], 2 * self.back(s) + 1, self.ring_send, recv)
        self.copy(self.blocks.at[self.mine], self.sibling, self.sib_send, self.sib_recv.at[0])

    def step(self, k):
        base = 2 * self.source(k)
        whole = self.blocks.at[base + self.core if k == self.half else pl.ds(base, 2)]
        if k == self.half:
            for p in range(self.parts):
                wait_bytes(self.part(base + self.core, p), self.ring_recv.at[k, p])
        elif k not in self.leg:
            wait_bytes(whole, self.ring_recv.at[k, 0])
        else:
            leg = self.leg[k]
            there = k + leg
            for p in range(self.parts):
                for h in range(2):
                    at = h * self.parts + p
                    wait_bytes(self.part(base + h, p), self.ring_recv.at[k, at])
                    if there < self.half:
                        recv = self.ring_recv.at[there, at]
                        self.copy(self.part(base + h, p), self.onward(leg), self.ring_send, recv)
                if there == self.half:
                    recv = self.ring_recv.at[there, p]
                    self.copy(self.part(base + self.core, p), self.onward(leg), self.ring_send, recv)
            for s in range(leg - 1, 0, -1):
                self.copy(whole, self.onward(s), self.ring_send, self.ring_recv.at[k + s, 0])
        self.copy(whole, self.sibling, self.sib_send, self.sib_recv.at[k])

    def steps(self, *ks):
        for k in sorted((k for k in ks if k <= self.half), key=self.order.index):
            self.step(k)

    def arrived(self, k):
        got = self.blocks.at[pl.ds(0, 1 if k == 0 or k == self.half else 2)]
        wait_bytes(got, self.sib_recv.at[k])

    def finish(self):
        wait_bytes(self.blocks.at[pl.ds(0, self.chips - 1)], self.ring_send)
        wait_bytes(self.blocks.at[pl.ds(0, self.chips)], self.sib_send)


class Carry:
    def __init__(self, chips, z, core, near, decays, refs, sems):
        self.chips, self.z, self.core, self.near = chips, z, core, near
        self.start, self.peer, self.joined, self.everything, self.found, self.into = refs
        self.peer_send, self.peer_recv, self.send1, self.recv1, self.send2, self.recv2, self.send3, self.recv3 = [
            sems.at[i] for i in range(8)
        ]
        self.rows = self.into.shape[1]
        self.decays = self.everything if decays is None else decays
        self.sent = self.rows + (decays is None)

    def put(self, state, decay):
        slices, rows = self.chips, self.rows
        for half in range(2):
            at = pl.ds(half * slices // 2, slices // 2)
            part = state[:, half * LANES : (half + 1) * LANES]
            self.start[at, pl.ds(0, rows), :] = part.reshape(slices // 2, rows, LANES)
            wide = jnp.broadcast_to(decay[:, half * LANES : (half + 1) * LANES], (8, LANES))
            self.start[at, pl.ds(rows, 8), :] = jnp.broadcast_to(wide[None], (slices // 2, 8, LANES))

    def hand(self):
        @pl.when(self.core == self.near)
        def _():
            pltpu.make_async_remote_copy(
                src_ref=self.start,
                dst_ref=self.peer,
                send_sem=self.peer_send,
                recv_sem=self.peer_recv,
                device_id={"ctx": 2 * self.z + 1 - self.near},
                device_id_type=MESH,
            ).start()
            self.peer[:, pl.ds(0, self.rows), :] = jnp.zeros((self.chips, self.rows, LANES), F32)
            self.peer[:, pl.ds(self.rows, 8), :] = jnp.ones((self.chips, 8, LANES), F32)

    def send(self):
        rows = self.rows

        @pl.when(self.core != self.near)
        def _():
            wait_bytes(self.peer, self.peer_recv)
            decay = self.start[:, rows : rows + 1, :]
            self.joined[:, pl.ds(0, rows), :] = self.start[:, 0:rows, :] + decay * self.peer[:, 0:rows, :]
            self.joined[:, pl.ds(rows, 8), :] = decay * self.peer[:, rows : rows + 8, :]

            def copy(chip):
                return dict(
                    src_ref=self.joined.at[chip, pl.ds(0, self.sent)],
                    dst_ref=self.everything.at[self.z, pl.ds(0, self.sent)],
                )

            def to(i, carry):
                chip = far_first(self.z, i, self.chips)
                pltpu.make_async_remote_copy(
                    **copy(chip),
                    send_sem=self.send1,
                    recv_sem=self.recv1,
                    device_id={"ctx": 2 * chip},
                    device_id_type=MESH,
                ).start()
                return carry

            lax.fori_loop(0, self.chips - 1, to, 0)
            if self.near == 1:
                pltpu.make_async_copy(*copy(self.z).values(), self.recv1).start()
            else:
                pltpu.make_async_remote_copy(
                    **copy(self.z),
                    send_sem=self.send1,
                    recv_sem=self.recv1,
                    device_id={"ctx": 2 * self.z},
                    device_id_type=MESH,
                ).start()

    def work(self):
        count, rows = self.chips, self.rows

        @pl.when(self.core == 0)
        def _():
            wait_bytes(self.everything.at[:, pl.ds(0, self.sent)], self.recv1)
            before = jnp.zeros((rows, LANES), F32)
            for k in range(count):
                at = count - 1 - k if self.near == 1 else k
                self.found[at] = before.astype(BF16)
                decay = jnp.broadcast_to(self.decays[at, rows : rows + 1, :], (rows, LANES))
                before = decay * before + self.everything[at, 0:rows, :]

            def copy(chip):
                return pltpu.make_async_remote_copy(
                    src_ref=self.found.at[chip],
                    dst_ref=self.into.at[self.z],
                    send_sem=self.send2,
                    recv_sem=self.recv2,
                    device_id={"ctx": 2 * chip + self.near},
                    device_id_type=MESH,
                )

            def to(i, carry):
                copy(far_first(self.z, i, count)).start()
                return carry

            lax.fori_loop(0, count - 1, to, 0)
            if self.near == 1:
                copy(self.z).start()
            else:
                pltpu.make_async_copy(self.found.at[self.z], self.into.at[self.z], self.recv2).start()

    def result(self):
        @pl.when(self.core == self.near)
        def _():
            wait_bytes(self.into, self.recv2)
            pltpu.make_async_remote_copy(
                src_ref=self.into,
                dst_ref=self.into,
                send_sem=self.send3,
                recv_sem=self.recv3,
                device_id={"ctx": 2 * self.z + 1 - self.near},
                device_id_type=MESH,
            ).start()

        @pl.when(self.core != self.near)
        def _():
            wait_bytes(self.into, self.recv3)

        halves = []
        for half in range(2):
            at = pl.ds(half * self.chips // 2, self.chips // 2)
            peer = self.peer[at]
            decay = peer[:, self.rows : self.rows + 1, :]
            part = decay * self.into[at].astype(F32) + peer[:, 0 : self.rows, :]
            halves.append(part.reshape(LANES, LANES))
        return split(jnp.concatenate(halves, axis=1))

    def finish(self):
        @pl.when(self.core == self.near)
        def _():
            wait_bytes(self.start, self.peer_send)
            wait_bytes(self.into, self.send3)

        @pl.when(self.core != self.near)
        def _():
            wait_bytes(self.joined.at[pl.ds(0, self.chips - self.near), pl.ds(0, self.sent)], self.send1)

        @pl.when(self.core == 0)
        def _():
            wait_bytes(self.found.at[pl.ds(0, self.chips - 1 + self.near)], self.send2)


class Total:
    def __init__(self, peers, tp, part, taken, share, full, sems):
        self.peers, self.tp = peers, tp
        self.part, self.taken, self.share, self.full = part, taken, share, full
        self.send1, self.recv1, self.send2, self.recv2 = [sems.at[i] for i in range(4)]

    def send(self, value):
        self.part[...] = value.reshape(self.part.shape)

        def to(i, carry):
            there = far_first(self.tp, i, self.peers)
            pltpu.make_async_remote_copy(
                src_ref=self.part.at[there],
                dst_ref=self.taken.at[self.tp],
                send_sem=self.send1,
                recv_sem=self.recv1,
                device_id={"tp": there},
                device_id_type=MESH,
            ).start()
            return carry

        lax.fori_loop(0, self.peers - 1, to, 0)
        pltpu.make_async_copy(self.part.at[self.tp], self.taken.at[self.tp], self.recv1).start()

    def add(self):
        wait_bytes(self.taken, self.recv1)
        total = self.taken[0]
        for k in range(1, self.peers):
            total = total + self.taken[k]
        self.share[...] = total

        def to(i, carry):
            there = far_first(self.tp, i, self.peers)
            pltpu.make_async_remote_copy(
                src_ref=self.share,
                dst_ref=self.full.at[self.tp],
                send_sem=self.send2,
                recv_sem=self.recv2,
                device_id={"tp": there},
                device_id_type=MESH,
            ).start()
            return carry

        lax.fori_loop(0, self.peers - 1, to, 0)
        pltpu.make_async_copy(self.share, self.full.at[self.tp], self.recv2).start()

    def result(self):
        wait_bytes(self.full, self.recv2)
        return self.full[...].reshape(LANES, LANES)

    def finish(self):
        wait_bytes(self.part.at[pl.ds(0, self.peers - 1)], self.send1)
        wait_bytes(self.full.at[pl.ds(0, self.peers - 1)], self.send2)


class Columns:
    def __init__(self, chips, peers, z, core, tp, inputs, stage, cols, sems):
        self.chips, self.peers = chips, peers
        self.z, self.core, self.tp = z, core, tp
        self.inputs, self.stage, self.cols = inputs, stage, cols
        self.send1, self.recv1, self.send2, self.recv2, self.send3, self.recv3 = [
            sems.at[i] for i in range(6)
        ]
        self.share = 2 * LANES // peers
        self.sender = lax.div(tp * self.share, LANES)
        self.row = pl.multiple_of(lax.rem(tp * self.share, LANES), self.share)

    def send(self):
        @pl.when(self.core == self.sender)
        def _():
            def block(chip):
                at = pl.multiple_of(chip * 2 * LANES, 2 * LANES)
                return self.inputs.at[pl.ds(self.row, self.share), pl.ds(at, 2 * LANES)]

            def to(i, carry):
                chip = far_first(self.z, i, self.chips)
                pltpu.make_async_remote_copy(
                    src_ref=block(chip),
                    dst_ref=self.stage.at[self.z],
                    send_sem=self.send1,
                    recv_sem=self.recv1,
                    device_id={"ctx": 2 * chip + self.core},
                    device_id_type=MESH,
                ).start()
                return carry

            lax.fori_loop(0, self.chips - 1, to, 0)
            pltpu.make_async_copy(block(self.z), self.stage.at[self.z], self.recv1).start()

    def share_out(self):
        @pl.when(self.core == self.sender)
        def _():
            wait_bytes(self.stage, self.recv1)

            def half(core):
                at = pl.multiple_of(core * LANES, LANES)
                return self.stage.at[:, :, pl.ds(at, LANES)]

            pltpu.make_async_remote_copy(
                src_ref=half(1 - self.core),
                dst_ref=self.cols.at[:, self.tp],
                send_sem=self.send2,
                recv_sem=self.recv2,
                device_id={"ctx": 2 * self.z + 1 - self.core},
                device_id_type=MESH,
            ).start()
            pltpu.make_async_copy(half(self.core), self.cols.at[:, self.tp], self.recv2).start()

    def spread(self):
        mine = self.cols.at[:, self.tp]
        wait_bytes(mine, self.recv2)

        def to(i, carry):
            there = far_first(self.tp, i, self.peers)
            pltpu.make_async_remote_copy(
                src_ref=mine,
                dst_ref=mine,
                send_sem=self.send3,
                recv_sem=self.recv3,
                device_id={"tp": there},
                device_id_type=MESH,
            ).start()
            return carry

        lax.fori_loop(0, self.peers - 1, to, 0)

    def arrived(self):
        wait_bytes(self.cols.at[:, pl.ds(0, self.peers - 1)], self.recv3)

    def finish(self):
        @pl.when(self.core == self.sender)
        def _():
            sent = self.inputs.at[pl.ds(0, self.share), pl.ds(0, (self.chips - 1) * 2 * LANES)]
            wait_bytes(sent, self.send1)
            wait_bytes(self.cols.at[:, self.tp], self.send2)

        wait_bytes(self.cols.at[:, pl.ds(0, self.peers - 1)], self.send3)


def kernel(
    chips, peers,
    inputs_hbm, w_hbm, b_hbm, c_hbm, ld_hbm, skip, dout_hbm,
    dw_ref, db_ref, dc_ref,
    inputs, b_ref, c_ref, ld_ref, dout_ref,
    gw, gg, stage, cols,
    a_start, a_peer, a_joined, a_all, a_found, a_into,
    s_start, s_peer, s_joined, s_all, s_found, s_into,
    b_part, b_taken, b_share, b_full,
    c_part, c_taken, c_share, c_full,
    ring_send, ring_recv, sib_recv, carry_sems, total_sems, cols_sems, fetch_sems, wave_sems,
):
    ctx, tp = lax.axis_index("ctx"), lax.axis_index("tp")
    devices = 2 * chips
    z, core = lax.div(ctx, 2), lax.rem(ctx, 2)
    heads = 4

    barrier = pltpu.get_barrier_semaphore()

    near_chips = [k % chips for k in (1, -1, 2, -2)]
    side = 4 if peers == 16 else 1
    rest = peers // side
    row, place = lax.div(tp, rest), lax.rem(tp, rest)
    in_row = [row * rest + lax.rem(place + k, rest) for k in range(1, rest)]
    in_column = [lax.rem(row + k, side) * rest + place for k in range(1, side)]
    near = [{"ctx": 2 * lax.rem(z + k, chips) + c} for k in near_chips for c in range(2)]
    near += [{"ctx": 2 * z + 1 - core}] + [{"tp": t} for t in in_row + in_column]

    def greet(sem, who):
        for device in who:
            pl.semaphore_signal(sem, inc=1, device_id=device, device_id_type=MESH)
        return len(who)

    greeted = greet(barrier, near)
    fetches = [
        pltpu.make_async_copy(there, here, fetch_sems.at[i])
        for i, (there, here) in enumerate(
            [
                (w_hbm, gw.at[ctx]),
                (ld_hbm, ld_ref),
                (c_hbm, c_ref),
                (dout_hbm, dout_ref),
                (b_hbm, b_ref),
                (inputs_hbm, inputs),
            ]
        )
    ]
    for fetch in fetches:
        fetch.start()

    ring_w = Ring(
        chips, *RING_W, z, core, gw, ring_send.at[0], ring_send.at[1], ring_recv.at[0], sib_recv.at[0]
    )
    ring_g = Ring(
        chips, *RING_G, z, core, gg, ring_send.at[2], ring_send.at[3], ring_recv.at[1], sib_recv.at[1]
    )
    adjoint = Carry(
        chips, z, core, 1, None, (a_start, a_peer, a_joined, a_all, a_found, a_into), carry_sems.at[0]
    )
    state = Carry(
        chips, z, core, 0, a_all, (s_start, s_peer, s_joined, s_all, s_found, s_into), carry_sems.at[1]
    )
    total_b = Total(peers, tp, b_part, b_taken, b_share, b_full, total_sems.at[0])
    columns = Columns(chips, peers, z, core, tp, inputs, stage, cols, cols_sems)
    total_c = Total(peers, tp, c_part, c_taken, c_share, c_full, total_sems.at[1])

    fetches[0].wait()
    pl.semaphore_wait(barrier, greeted)
    ring_w.begin()

    met_row = greet(wave_sems.at[0], [{"tp": t} for t in in_row])

    def vouch(reach):
        at = wave_sems.at[1 if reach == 2 else 2]
        return at, greet(at, [{"ctx": 2 * lax.rem(z + k, chips) + core} for k in (reach, chips - reach)])

    met = vouch(2)

    rows = lax.broadcasted_iota(jnp.int32, (LANES, LANES), 0)
    lanes = lax.broadcasted_iota(jnp.int32, (LANES, LANES), 1)
    upper = (rows <= lanes).astype(F32)
    first, first_rows = lanes < LANES // 2, rows < LANES // 2
    for fetch in fetches[1:5]:
        fetch.wait()
    cumulative_t = []
    for q in range(2):
        pair = [jnp.broadcast_to(ld_ref[2 * q + i : 2 * q + i + 1, :], (LANES, LANES)) for i in range(2)]
        cumulative_t.append(dot(jnp.where(first_rows, pair[0], pair[1]), upper, precision=HIGHEST))
    cumulative = jnp.concatenate([part.T for part in cumulative_t], axis=1)
    pl.semaphore_wait(*met)
    if chips > 8:
        met = vouch(4)
    block_log = cumulative[LANES - 1 : LANES, :]
    block_decay = jnp.exp(block_log)
    to_end = jnp.exp(block_log - cumulative)
    from_start = jnp.exp(cumulative)
    b, c, dout = b_ref[...], c_ref[...], dout_ref[...]
    b_t = b.astype(F32).T.astype(BF16)
    c_t = c.astype(F32).T.astype(BF16)
    dout_wide = dout.astype(F32)
    started = split(from_start * dout_wide)
    adjoint.put(dot_split(c_t, started), block_decay)

    adjoint.hand()
    if chips > 8:
        pl.semaphore_wait(*met)
    pl.semaphore_wait(wave_sems.at[0], met_row)
    fetches[5].wait()
    adjoint.send()
    ring_w.steps(1, 2)
    columns.send()

    def project(total, chip):
        at = pl.multiple_of(chip * 2 * LANES, 2 * LANES)
        block = gw[pl.ds(2 * chip, 2)].reshape(2 * LANES, -1)
        return total + dot(inputs[:, pl.ds(at, 2 * LANES)], block)

    def project_both(total, k):
        total = project(total, ring_w.source(k))
        ring_w.arrived(k)
        return project(total, ring_w.sibling_source(k))

    scores_t = dot(b, c, SECOND_T)
    later = lanes >= rows
    within, within_t = [], []
    for h in range(heads):
        q, side = h // 2, (h % 2) * (LANES // 2)
        column = cumulative[:, q * LANES + side : q * LANES + side + 1]
        row = cumulative_t[q][side : side + 1, :]
        within.append(jnp.where(rows >= lanes, jnp.exp(jnp.where(rows >= lanes, column - row, 0.0)), 0.0))
        within_t.append(jnp.where(later, jnp.exp(jnp.where(later, row - column, 0.0)), 0.0))
    local = []
    for q in range(2):
        pair = dout[:, q * LANES : (q + 1) * LANES]
        sides = [dot((within_t[2 * q + i] * scores_t).astype(BF16), pair) for i in range(2)]
        scale = jnp.where(first, skip[2 * q], skip[2 * q + 1])
        local.append(jnp.where(first, sides[0], sides[1]) + scale * pair.astype(F32))
    local = jnp.concatenate(local, axis=1)

    ring_w.steps(3, 4)
    ring_w.arrived(0)
    projected = project(jnp.zeros((LANES, 2 * LANES), F32), z)
    for k in (1, 2):
        projected = project_both(projected, k)
    ring_w.steps(5, 6)
    adjoint.work()
    columns.share_out()
    for k in range(3, chips // 2 - 1):
        projected = project_both(projected, k)
    columns.spread()
    ring_w.steps(7, 8)

    projected = project_both(projected, chips // 2 - 1)
    ring_w.arrived(chips // 2)
    projected = project(projected, ring_w.source(chips // 2))
    values = projected.astype(BF16)
    ended = split(to_end * values.astype(F32))
    state.put(dot_split(b_t, ended), block_decay)
    state.hand()
    state.send()

    adjoint_in = adjoint.result()
    grad_values = local + to_end * dot_split(b, adjoint_in)
    gg[ctx] = grad_values.astype(BF16)
    ring_g.begin()

    d_b = carried(ended, adjoint_in)
    d_c = jnp.zeros((LANES, LANES), F32)
    for h in range(heads):
        q = h // 2
        mine = first if h % 2 == 0 else jnp.logical_not(first)
        part = values[:, q * LANES : (q + 1) * LANES]
        part = jnp.where(mine, part.astype(F32), 0.0).astype(BF16)
        pair = dout[:, q * LANES : (q + 1) * LANES]
        weights = (within[h] * dot(pair, part, SECOND_T)).astype(BF16)
        weights_t = (within_t[h] * dot(part, pair, SECOND_T)).astype(BF16)
        d_c = d_c + dot(weights, b)
        d_b = d_b + dot(weights_t, c)
    total_b.send(d_b)
    ring_g.steps(1, 2)
    state.work()
    ring_g.steps(3, 4)
    total_b.add()
    ring_g.steps(5, 6)
    state_in = state.result()
    d_c = d_c + carried(started, state_in)
    total_c.send(d_c)

    def project_back(total, chip):
        return total + dot(
            cols[chip].reshape(2 * LANES, LANES).astype(F32).T.astype(BF16),
            gg[pl.ds(2 * chip, 2)].reshape(2 * LANES, -1),
        )

    def back_both(total, k):
        total = project_back(total, ring_g.source(k))
        ring_g.arrived(k)
        return project_back(total, ring_g.sibling_source(k))

    columns.arrived()
    ring_g.arrived(0)
    grad_w = project_back(jnp.zeros((LANES, 2 * LANES), F32), z)
    ring_g.steps(7, 8)
    for k in range(1, chips // 2 - 1):
        grad_w = back_both(grad_w, k)
    total_c.add()
    grad_w = back_both(grad_w, chips // 2 - 1)
    ring_g.arrived(chips // 2)
    dw_ref[...] = project_back(grad_w, ring_g.source(chips // 2))
    db_ref[...] = total_b.result()
    dc_ref[...] = total_c.result()

    ring_w.finish()
    ring_g.finish()
    adjoint.finish()
    state.finish()
    total_b.finish()
    total_c.finish()
    columns.finish()


def solution(mesh):
    devices, peers = mesh.shape["ctx"], mesh.shape["tp"]
    chips = devices // 2

    def per_device(inputs, w_in, b_in, c_in, log_decay, skip, d_out):
        tokens, width = d_out.shape
        rows = LANES // (chips // 2)
        vmem, hbm = pl.BlockSpec(memory_space=pltpu.VMEM), pl.BlockSpec(memory_space=pltpu.HBM)
        def carry_scratch(sent):
            return [
                pltpu.VMEM((chips, rows + 8, LANES), F32),
                pltpu.VMEM((chips, rows + 8, LANES), F32),
                pltpu.VMEM((chips, rows + 8, LANES), F32),
                pltpu.VMEM((chips, sent, LANES), F32),
                pltpu.VMEM((chips, rows, LANES), BF16),
                pltpu.VMEM((chips, rows, LANES), BF16),
            ]

        total_scratch = [
            pltpu.VMEM((peers, tokens // peers, LANES), F32),
            pltpu.VMEM((peers, tokens // peers, LANES), F32),
            pltpu.VMEM((tokens // peers, LANES), F32),
            pltpu.VMEM((peers, tokens // peers, LANES), F32),
        ]
        half = chips // 2
        return pl.pallas_call(
            functools.partial(kernel, chips, peers),
            out_shape=(
                pltpu.VMEM(w_in.shape, F32),
                pltpu.VMEM(b_in.shape, F32),
                pltpu.VMEM(c_in.shape, F32),
            ),
            in_specs=[hbm] * 5 + [pl.BlockSpec(memory_space=pltpu.SMEM), hbm],
            out_specs=(vmem, vmem, vmem),
            scratch_shapes=[
                pltpu.VMEM(inputs.shape, BF16),
                pltpu.VMEM(b_in.shape, BF16),
                pltpu.VMEM(c_in.shape, BF16),
                pltpu.VMEM(log_decay.shape[::-1], F32),
                pltpu.VMEM(d_out.shape, BF16),
                pltpu.VMEM((devices, tokens, width), BF16),
                pltpu.VMEM((devices, tokens, width), BF16),
                pltpu.VMEM((chips, 2 * tokens // peers, 2 * LANES), BF16),
                pltpu.VMEM((chips, peers, 2 * tokens // peers, LANES), BF16),
            ]
            + carry_scratch(rows + 8)
            + carry_scratch(rows)
            + total_scratch * 2
            + [
                pltpu.SemaphoreType.DMA((4,)),
                pltpu.SemaphoreType.DMA((2, half + 1, 2 * max(RING_W[1], RING_G[1]))),
                pltpu.SemaphoreType.DMA((2, half + 1)),
                pltpu.SemaphoreType.DMA((2, 8)),
                pltpu.SemaphoreType.DMA((2, 4)),
                pltpu.SemaphoreType.DMA((6,)),
                pltpu.SemaphoreType.DMA((6,)),
                pltpu.SemaphoreType.REGULAR((3,)),
            ],
            compiler_params=pltpu.CompilerParams(
                collective_id=0, has_side_effects=True, vmem_limit_bytes=60 * 1024 * 1024
            ),
        )(inputs, w_in, b_in, c_in, log_decay.T, skip, d_out)

    return jax.shard_map(
        per_device,
        mesh=mesh,
        in_specs=(
            P("ctx", None),
            P("ctx", "tp"),
            P("ctx", None),
            P("ctx", None),
            P("ctx", "tp"),
            P("tp"),
            P("ctx", "tp"),
        ),
        out_specs=(P("ctx", "tp"), P("ctx", None), P("ctx", None)),
        check_vma=False,
    )
```

```python
import functools

import jax
import jax.numpy as jnp
from jax import lax
from jax.experimental import pallas as pl
from jax.experimental.pallas import tpu as pltpu
from jax.sharding import PartitionSpec as P

F32 = jnp.float32
BF16 = jnp.bfloat16
MESH = pl.DeviceIdType.MESH
HIGHEST = lax.Precision.HIGHEST
LANES = 128
RING_W, RING_G = ((2,), 2), ((2,), 2)
PLAIN = ((1,), (0,))
SECOND_T = ((1,), (1,))


def dot(a, b, dims=PLAIN, precision=None):
    return lax.dot_general(a, b, (dims, ((), ())), precision=precision, preferred_element_type=F32)


def split(x):
    high = x.astype(BF16)
    return high, (x - high.astype(F32)).astype(BF16)


def dot_split(a, b_pair):
    return dot(a, b_pair[0]) + dot(a, b_pair[1])


def carried(a_pair, b_pair):
    return sum(dot(a_pair[i], b_pair[j], SECOND_T) for i, j in ((0, 0), (0, 1), (1, 0)))


def wait_bytes(ref, sem):
    pltpu.make_async_copy(ref, ref, sem).wait()


def far_first(place, i, count):
    aside = lax.div(i + 1, 2)
    return lax.rem(place + count // 2 + jnp.where(lax.rem(i, 2) == 1, count - aside, aside), count)


class Ring:
    def __init__(self, chips, legs, parts, z, core, blocks, ring_send, sib_send, ring_recv, sib_recv):
        self.chips, self.parts, self.half = chips, parts, chips // 2
        self.leg, self.order, at = {}, [], 0
        while at < self.half:
            self.leg[at] = min(legs[len(self.leg) % len(legs)], self.half - at)
            self.order += range(at + self.leg[at], at, -1)
            at += self.leg[at]
        self.z, self.core, self.blocks = z, core, blocks
        self.ring_send, self.sib_send = ring_send, sib_send
        self.ring_recv, self.sib_recv = ring_recv, sib_recv
        self.sibling, self.mine = 2 * z + 1 - core, 2 * z + core
        self.rows = blocks.shape[1] // parts

    def copy(self, ref, to, send, recv):
        pltpu.make_async_remote_copy(
            src_ref=ref, dst_ref=ref, send_sem=send, recv_sem=recv, device_id={"ctx": to}, device_id_type=MESH
        ).start()

    def part(self, block, p):
        return self.blocks.at[block, pl.ds(p * self.rows, self.rows)]

    def back(self, k):
        return lax.rem(self.z + (self.chips - k), self.chips)

    def ahead(self, k):
        return lax.rem(self.z + k, self.chips)

    def source(self, k):
        return jnp.where(self.core == 0, self.back(k), self.ahead(k))

    def sibling_source(self, k):
        return jnp.where(self.core == 0, self.ahead(k), self.back(k))

    def onward(self, k):
        return 2 * self.sibling_source(k) + self.core

    def begin(self):
        leg = self.leg[0]
        for p in range(self.parts):
            recv = self.ring_recv.at[leg, self.core * self.parts + p]
            self.copy(self.part(self.mine, p), 2 * self.ahead(leg), self.ring_send, recv)
            self.copy(self.part(self.mine, p), 2 * self.back(leg) + 1, self.ring_send, recv)
        for s in range(leg - 1, 0, -1):
            recv = self.ring_recv.at[s, 0]
            self.copy(self.blocks.at[self.mine], 2 * self.ahead(s), self.ring_send, recv)
            self.copy(self.blocks.at[self.mine], 2 * self.back(s) + 1, self.ring_send, recv)
        self.copy(self.blocks.at[self.mine], self.sibling, self.sib_send, self.sib_recv.at[0])

    def step(self, k):
        base = 2 * self.source(k)
        whole = self.blocks.at[base + self.core if k == self.half else pl.ds(base, 2)]
        if k == self.half:
            for p in range(self.parts):
                wait_bytes(self.part(base + self.core, p), self.ring_recv.at[k, p])
        elif k not in self.leg:
            wait_bytes(whole, self.ring_recv.at[k, 0])
        else:
            leg = self.leg[k]
            there = k + leg
            for p in range(self.parts):
                for h in range(2):
                    at = h * self.parts + p
                    wait_bytes(self.part(base + h, p), self.ring_recv.at[k, at])
                    if there < self.half:
                        recv = self.ring_recv.at[there, at]
                        self.copy(self.part(base + h, p), self.onward(leg), self.ring_send, recv)
                if there == self.half:
                    recv = self.ring_recv.at[there, p]
                    self.copy(self.part(base + self.core, p), self.onward(leg), self.ring_send, recv)
            for s in range(leg - 1, 0, -1):
                self.copy(whole, self.onward(s), self.ring_send, self.ring_recv.at[k + s, 0])
        self.copy(whole, self.sibling, self.sib_send, self.sib_recv.at[k])

    def steps(self, *ks):
        for k in sorted((k for k in ks if k <= self.half), key=self.order.index):
            self.step(k)

    def arrived(self, k):
        got = self.blocks.at[pl.ds(0, 1 if k == 0 or k == self.half else 2)]
        wait_bytes(got, self.sib_recv.at[k])

    def finish(self):
        wait_bytes(self.blocks.at[pl.ds(0, self.chips - 1)], self.ring_send)
        wait_bytes(self.blocks.at[pl.ds(0, self.chips)], self.sib_send)


class Carry:
    def __init__(self, chips, z, core, near, decays, refs, sems):
        self.chips, self.z, self.core, self.near = chips, z, core, near
        self.start, self.peer, self.joined, self.everything, self.found, self.into = refs
        self.peer_send, self.peer_recv, self.send1, self.recv1, self.send2, self.recv2, self.send3, self.recv3 = [
            sems.at[i] for i in range(8)
        ]
        self.rows = self.into.shape[1]
        self.decays = self.everything if decays is None else decays
        self.sent = self.rows + (decays is None)

    def put(self, state, decay):
        slices, rows = self.chips, self.rows
        for half in range(2):
            at = pl.ds(half * slices // 2, slices // 2)
            part = state[:, half * LANES : (half + 1) * LANES]
            self.start[at, pl.ds(0, rows), :] = part.reshape(slices // 2, rows, LANES)
            wide = jnp.broadcast_to(decay[:, half * LANES : (half + 1) * LANES], (8, LANES))
            self.start[at, pl.ds(rows, 8), :] = jnp.broadcast_to(wide[None], (slices // 2, 8, LANES))

    def hand(self):
        @pl.when(self.core == self.near)
        def _():
            pltpu.make_async_remote_copy(
                src_ref=self.start,
                dst_ref=self.peer,
                send_sem=self.peer_send,
                recv_sem=self.peer_recv,
                device_id={"ctx": 2 * self.z + 1 - self.near},
                device_id_type=MESH,
            ).start()
            self.peer[:, pl.ds(0, self.rows), :] = jnp.zeros((self.chips, self.rows, LANES), F32)
            self.peer[:, pl.ds(self.rows, 8), :] = jnp.ones((self.chips, 8, LANES), F32)

    def send(self):
        rows = self.rows

        @pl.when(self.core != self.near)
        def _():
            wait_bytes(self.peer, self.peer_recv)
            decay = self.start[:, rows : rows + 1, :]
            both = self.start[:, 0:rows, :] + decay * self.peer[:, 0:rows, :]
            self.joined[:, pl.ds(0, rows), :] = both.astype(self.joined.dtype)
            if self.sent > rows:
                self.joined[:, pl.ds(rows, 8), :] = decay * self.peer[:, rows : rows + 8, :]

            def copy(chip):
                return dict(
                    src_ref=self.joined.at[chip, pl.ds(0, self.sent)],
                    dst_ref=self.everything.at[self.z, pl.ds(0, self.sent)],
                )

            def to(i, carry):
                chip = far_first(self.z, i, self.chips)
                pltpu.make_async_remote_copy(
                    **copy(chip),
                    send_sem=self.send1,
                    recv_sem=self.recv1,
                    device_id={"ctx": 2 * chip},
                    device_id_type=MESH,
                ).start()
                return carry

            lax.fori_loop(0, self.chips - 1, to, 0)
            if self.near == 1:
                pltpu.make_async_copy(*copy(self.z).values(), self.recv1).start()
            else:
                pltpu.make_async_remote_copy(
                    **copy(self.z),
                    send_sem=self.send1,
                    recv_sem=self.recv1,
                    device_id={"ctx": 2 * self.z},
                    device_id_type=MESH,
                ).start()

    def work(self):
        count, rows = self.chips, self.rows

        @pl.when(self.core == 0)
        def _():
            wait_bytes(self.everything.at[:, pl.ds(0, self.sent)], self.recv1)
            before = jnp.zeros((rows, LANES), F32)
            for k in range(count):
                at = count - 1 - k if self.near == 1 else k
                self.found[at] = before.astype(BF16)
                decay = jnp.broadcast_to(self.decays[at, rows : rows + 1, :], (rows, LANES))
                before = decay * before + self.everything[at, 0:rows, :].astype(F32)

            def copy(chip):
                return pltpu.make_async_remote_copy(
                    src_ref=self.found.at[chip],
                    dst_ref=self.into.at[self.z],
                    send_sem=self.send2,
                    recv_sem=self.recv2,
                    device_id={"ctx": 2 * chip + self.near},
                    device_id_type=MESH,
                )

            def to(i, carry):
                copy(far_first(self.z, i, count)).start()
                return carry

            lax.fori_loop(0, count - 1, to, 0)
            if self.near == 1:
                copy(self.z).start()
            else:
                pltpu.make_async_copy(self.found.at[self.z], self.into.at[self.z], self.recv2).start()

    def result(self):
        @pl.when(self.core == self.near)
        def _():
            wait_bytes(self.into, self.recv2)
            pltpu.make_async_remote_copy(
                src_ref=self.into,
                dst_ref=self.into,
                send_sem=self.send3,
                recv_sem=self.recv3,
                device_id={"ctx": 2 * self.z + 1 - self.near},
                device_id_type=MESH,
            ).start()

        @pl.when(self.core != self.near)
        def _():
            wait_bytes(self.into, self.recv3)

        halves = []
        for half in range(2):
            at = pl.ds(half * self.chips // 2, self.chips // 2)
            peer = self.peer[at]
            decay = peer[:, self.rows : self.rows + 1, :]
            part = decay * self.into[at].astype(F32) + peer[:, 0 : self.rows, :]
            halves.append(part.reshape(LANES, LANES))
        return split(jnp.concatenate(halves, axis=1))

    def finish(self):
        @pl.when(self.core == self.near)
        def _():
            wait_bytes(self.start, self.peer_send)
            wait_bytes(self.into, self.send3)

        @pl.when(self.core != self.near)
        def _():
            wait_bytes(self.joined.at[pl.ds(0, self.chips - self.near), pl.ds(0, self.sent)], self.send1)

        @pl.when(self.core == 0)
        def _():
            wait_bytes(self.found.at[pl.ds(0, self.chips - 1 + self.near)], self.send2)


class Total:
    def __init__(self, peers, tp, part, taken, share, full, sems):
        self.peers, self.tp = peers, tp
        self.part, self.taken, self.share, self.full = part, taken, share, full
        self.send1, self.recv1, self.send2, self.recv2 = [sems.at[i] for i in range(4)]

    def send(self, value):
        self.part[...] = value.reshape(self.part.shape)

        def to(i, carry):
            there = far_first(self.tp, i, self.peers)
            pltpu.make_async_remote_copy(
                src_ref=self.part.at[there],
                dst_ref=self.taken.at[self.tp],
                send_sem=self.send1,
                recv_sem=self.recv1,
                device_id={"tp": there},
                device_id_type=MESH,
            ).start()
            return carry

        lax.fori_loop(0, self.peers - 1, to, 0)
        pltpu.make_async_copy(self.part.at[self.tp], self.taken.at[self.tp], self.recv1).start()

    def add(self):
        wait_bytes(self.taken, self.recv1)
        total = self.taken[0]
        for k in range(1, self.peers):
            total = total + self.taken[k]
        self.share[...] = total

        def to(i, carry):
            there = far_first(self.tp, i, self.peers)
            pltpu.make_async_remote_copy(
                src_ref=self.share,
                dst_ref=self.full.at[self.tp],
                send_sem=self.send2,
                recv_sem=self.recv2,
                device_id={"tp": there},
                device_id_type=MESH,
            ).start()
            return carry

        lax.fori_loop(0, self.peers - 1, to, 0)
        pltpu.make_async_copy(self.share, self.full.at[self.tp], self.recv2).start()

    def result(self):
        wait_bytes(self.full, self.recv2)
        return self.full[...].reshape(LANES, LANES)

    def finish(self):
        wait_bytes(self.part.at[pl.ds(0, self.peers - 1)], self.send1)
        wait_bytes(self.full.at[pl.ds(0, self.peers - 1)], self.send2)


class Columns:
    def __init__(self, chips, peers, z, core, tp, inputs, stage, cols, sems):
        self.chips, self.peers = chips, peers
        self.z, self.core, self.tp = z, core, tp
        self.inputs, self.stage, self.cols = inputs, stage, cols
        self.send1, self.recv1, self.send2, self.recv2, self.send3, self.recv3 = [
            sems.at[i] for i in range(6)
        ]
        self.share = 2 * LANES // peers
        self.sender = lax.div(tp * self.share, LANES)
        self.row = pl.multiple_of(lax.rem(tp * self.share, LANES), self.share)

    def send(self):
        @pl.when(self.core == self.sender)
        def _():
            def block(chip):
                at = pl.multiple_of(chip * 2 * LANES, 2 * LANES)
                return self.inputs.at[pl.ds(self.row, self.share), pl.ds(at, 2 * LANES)]

            def to(i, carry):
                chip = far_first(self.z, i, self.chips)
                pltpu.make_async_remote_copy(
                    src_ref=block(chip),
                    dst_ref=self.stage.at[self.z],
                    send_sem=self.send1,
                    recv_sem=self.recv1,
                    device_id={"ctx": 2 * chip + self.core},
                    device_id_type=MESH,
                ).start()
                return carry

            lax.fori_loop(0, self.chips - 1, to, 0)
            pltpu.make_async_copy(block(self.z), self.stage.at[self.z], self.recv1).start()

    def share_out(self):
        @pl.when(self.core == self.sender)
        def _():
            wait_bytes(self.stage, self.recv1)

            def half(core):
                at = pl.multiple_of(core * LANES, LANES)
                return self.stage.at[:, :, pl.ds(at, LANES)]

            pltpu.make_async_remote_copy(
                src_ref=half(1 - self.core),
                dst_ref=self.cols.at[:, self.tp],
                send_sem=self.send2,
                recv_sem=self.recv2,
                device_id={"ctx": 2 * self.z + 1 - self.core},
                device_id_type=MESH,
            ).start()
            pltpu.make_async_copy(half(self.core), self.cols.at[:, self.tp], self.recv2).start()

    def spread(self):
        mine = self.cols.at[:, self.tp]
        wait_bytes(mine, self.recv2)

        def to(i, carry):
            there = far_first(self.tp, i, self.peers)
            pltpu.make_async_remote_copy(
                src_ref=mine,
                dst_ref=mine,
                send_sem=self.send3,
                recv_sem=self.recv3,
                device_id={"tp": there},
                device_id_type=MESH,
            ).start()
            return carry

        lax.fori_loop(0, self.peers - 1, to, 0)

    def arrived(self):
        wait_bytes(self.cols.at[:, pl.ds(0, self.peers - 1)], self.recv3)

    def finish(self):
        @pl.when(self.core == self.sender)
        def _():
            sent = self.inputs.at[pl.ds(0, self.share), pl.ds(0, (self.chips - 1) * 2 * LANES)]
            wait_bytes(sent, self.send1)
            wait_bytes(self.cols.at[:, self.tp], self.send2)

        wait_bytes(self.cols.at[:, pl.ds(0, self.peers - 1)], self.send3)


def kernel(
    chips, peers,
    inputs_hbm, w_hbm, b_hbm, c_hbm, ld_hbm, skip, dout_hbm,
    dw_ref, db_ref, dc_ref,
    inputs, b_ref, c_ref, ld_ref, dout_ref,
    gw, gg, stage, cols,
    a_start, a_peer, a_joined, a_all, a_found, a_into,
    s_start, s_peer, s_joined, s_all, s_found, s_into,
    b_part, b_taken, b_share, b_full,
    c_part, c_taken, c_share, c_full,
    ring_send, ring_recv, sib_recv, carry_sems, total_sems, cols_sems, fetch_sems, wave_sems,
):
    ctx, tp = lax.axis_index("ctx"), lax.axis_index("tp")
    devices = 2 * chips
    z, core = lax.div(ctx, 2), lax.rem(ctx, 2)
    heads = 4

    barrier = pltpu.get_barrier_semaphore()

    near_chips = [k % chips for k in (1, -1, 2, -2)]
    side = 4 if peers == 16 else 1
    rest = peers // side
    row, place = lax.div(tp, rest), lax.rem(tp, rest)
    in_row = [row * rest + lax.rem(place + k, rest) for k in range(1, rest)]
    in_column = [lax.rem(row + k, side) * rest + place for k in range(1, side)]
    near = [{"ctx": 2 * lax.rem(z + k, chips) + c} for k in near_chips for c in range(2)]
    near += [{"ctx": 2 * z + 1 - core}] + [{"tp": t} for t in in_row + in_column]

    def greet(sem, who):
        for device in who:
            pl.semaphore_signal(sem, inc=1, device_id=device, device_id_type=MESH)
        return len(who)

    greeted = greet(barrier, near)
    fetches = [
        pltpu.make_async_copy(there, here, fetch_sems.at[i])
        for i, (there, here) in enumerate(
            [
                (w_hbm, gw.at[ctx]),
                (ld_hbm, ld_ref),
                (c_hbm, c_ref),
                (dout_hbm, dout_ref),
                (b_hbm, b_ref),
                (inputs_hbm, inputs),
            ]
        )
    ]
    for fetch in fetches:
        fetch.start()

    ring_w = Ring(
        chips, *RING_W, z, core, gw, ring_send.at[0], ring_send.at[1], ring_recv.at[0], sib_recv.at[0]
    )
    ring_g = Ring(
        chips, *RING_G, z, core, gg, ring_send.at[2], ring_send.at[3], ring_recv.at[1], sib_recv.at[1]
    )
    adjoint = Carry(
        chips, z, core, 1, None, (a_start, a_peer, a_joined, a_all, a_found, a_into), carry_sems.at[0]
    )
    state = Carry(
        chips, z, core, 0, a_all, (s_start, s_peer, s_joined, s_all, s_found, s_into), carry_sems.at[1]
    )
    total_b = Total(peers, tp, b_part, b_taken, b_share, b_full, total_sems.at[0])
    columns = Columns(chips, peers, z, core, tp, inputs, stage, cols, cols_sems)
    total_c = Total(peers, tp, c_part, c_taken, c_share, c_full, total_sems.at[1])

    fetches[0].wait()
    pl.semaphore_wait(barrier, greeted)
    ring_w.begin()

    met_row = greet(wave_sems.at[0], [{"tp": t} for t in in_row])

    def vouch(reach):
        at = wave_sems.at[1 if reach == 2 else 2]
        return at, greet(at, [{"ctx": 2 * lax.rem(z + k, chips) + core} for k in (reach, chips - reach)])

    met = vouch(2)

    rows = lax.broadcasted_iota(jnp.int32, (LANES, LANES), 0)
    lanes = lax.broadcasted_iota(jnp.int32, (LANES, LANES), 1)
    upper = (rows <= lanes).astype(F32)
    first, first_rows = lanes < LANES // 2, rows < LANES // 2
    for fetch in fetches[1:5]:
        fetch.wait()
    cumulative_t = []
    for q in range(2):
        pair = [jnp.broadcast_to(ld_ref[2 * q + i : 2 * q + i + 1, :], (LANES, LANES)) for i in range(2)]
        cumulative_t.append(dot(jnp.where(first_rows, pair[0], pair[1]), upper, precision=HIGHEST))
    cumulative = jnp.concatenate([part.T for part in cumulative_t], axis=1)
    pl.semaphore_wait(*met)
    if chips > 8:
        met = vouch(4)
    block_log = cumulative[LANES - 1 : LANES, :]
    block_decay = jnp.exp(block_log)
    to_end = jnp.exp(block_log - cumulative)
    from_start = jnp.exp(cumulative)
    b, c, dout = b_ref[...], c_ref[...], dout_ref[...]
    b_t = b.astype(F32).T.astype(BF16)
    c_t = c.astype(F32).T.astype(BF16)
    dout_wide = dout.astype(F32)
    started = split(from_start * dout_wide)
    adjoint.put(dot_split(c_t, started), block_decay)

    adjoint.hand()
    if chips > 8:
        pl.semaphore_wait(*met)
    pl.semaphore_wait(wave_sems.at[0], met_row)
    fetches[5].wait()
    adjoint.send()
    ring_w.steps(1, 2)
    columns.send()

    def project(total, chip):
        at = pl.multiple_of(chip * 2 * LANES, 2 * LANES)
        block = gw[pl.ds(2 * chip, 2)].reshape(2 * LANES, -1)
        return total + dot(inputs[:, pl.ds(at, 2 * LANES)], block)

    def project_both(total, k):
        total = project(total, ring_w.source(k))
        ring_w.arrived(k)
        return project(total, ring_w.sibling_source(k))

    scores_t = dot(b, c, SECOND_T)
    later = lanes >= rows
    within, within_t = [], []
    for h in range(heads):
        q, side = h // 2, (h % 2) * (LANES // 2)
        column = cumulative[:, q * LANES + side : q * LANES + side + 1]
        row = cumulative_t[q][side : side + 1, :]
        within.append(jnp.where(rows >= lanes, jnp.exp(jnp.where(rows >= lanes, column - row, 0.0)), 0.0))
        within_t.append(jnp.where(later, jnp.exp(jnp.where(later, row - column, 0.0)), 0.0))
    local = []
    for q in range(2):
        pair = dout[:, q * LANES : (q + 1) * LANES]
        sides = [dot((within_t[2 * q + i] * scores_t).astype(BF16), pair) for i in range(2)]
        scale = jnp.where(first, skip[2 * q], skip[2 * q + 1])
        local.append(jnp.where(first, sides[0], sides[1]) + scale * pair.astype(F32))
    local = jnp.concatenate(local, axis=1)

    ring_w.steps(3, 4)
    ring_w.arrived(0)
    projected = project(jnp.zeros((LANES, 2 * LANES), F32), z)
    for k in (1, 2):
        projected = project_both(projected, k)
    ring_w.steps(5, 6)
    adjoint.work()
    columns.share_out()
    for k in range(3, chips // 2 - 1):
        projected = project_both(projected, k)
    columns.spread()
    ring_w.steps(7, 8)

    projected = project_both(projected, chips // 2 - 1)
    ring_w.arrived(chips // 2)
    projected = project(projected, ring_w.source(chips // 2))
    values = projected.astype(BF16)
    ended = split(to_end * values.astype(F32))
    state.put(dot_split(b_t, ended), block_decay)
    state.hand()
    state.send()

    adjoint_in = adjoint.result()
    grad_values = local + to_end * dot_split(b, adjoint_in)
    gg[ctx] = grad_values.astype(BF16)
    ring_g.begin()

    d_b = carried(ended, adjoint_in)
    d_c = jnp.zeros((LANES, LANES), F32)
    for h in range(heads):
        q = h // 2
        mine = first if h % 2 == 0 else jnp.logical_not(first)
        part = values[:, q * LANES : (q + 1) * LANES]
        part = jnp.where(mine, part.astype(F32), 0.0).astype(BF16)
        pair = dout[:, q * LANES : (q + 1) * LANES]
        weights = (within[h] * dot(pair, part, SECOND_T)).astype(BF16)
        weights_t = (within_t[h] * dot(part, pair, SECOND_T)).astype(BF16)
        d_c = d_c + dot(weights, b)
        d_b = d_b + dot(weights_t, c)
    total_b.send(d_b)
    state.work()
    ring_g.steps(1, 2)
    ring_g.steps(3, 4)
    total_b.add()
    ring_g.steps(5, 6)
    state_in = state.result()
    d_c = d_c + carried(started, state_in)
    total_c.send(d_c)

    def project_back(total, chip):
        return total + dot(
            cols[chip].reshape(2 * LANES, LANES).astype(F32).T.astype(BF16),
            gg[pl.ds(2 * chip, 2)].reshape(2 * LANES, -1),
        )

    def back_both(total, k):
        total = project_back(total, ring_g.source(k))
        ring_g.arrived(k)
        return project_back(total, ring_g.sibling_source(k))

    columns.arrived()
    ring_g.arrived(0)
    grad_w = project_back(jnp.zeros((LANES, 2 * LANES), F32), z)
    ring_g.steps(7, 8)
    for k in range(1, chips // 2 - 1):
        grad_w = back_both(grad_w, k)
    total_c.add()
    grad_w = back_both(grad_w, chips // 2 - 1)
    ring_g.arrived(chips // 2)
    dw_ref[...] = project_back(grad_w, ring_g.source(chips // 2))
    db_ref[...] = total_b.result()
    dc_ref[...] = total_c.result()

    ring_w.finish()
    ring_g.finish()
    adjoint.finish()
    state.finish()
    total_b.finish()
    total_c.finish()
    columns.finish()


def solution(mesh):
    devices, peers = mesh.shape["ctx"], mesh.shape["tp"]
    chips = devices // 2

    def per_device(inputs, w_in, b_in, c_in, log_decay, skip, d_out):
        tokens, width = d_out.shape
        rows = LANES // (chips // 2)
        vmem, hbm = pl.BlockSpec(memory_space=pltpu.VMEM), pl.BlockSpec(memory_space=pltpu.HBM)
        def carry_scratch(sent, dtype):
            return [
                pltpu.VMEM((chips, rows + 8, LANES), F32),
                pltpu.VMEM((chips, rows + 8, LANES), F32),
                pltpu.VMEM((chips, sent, LANES), dtype),
                pltpu.VMEM((chips, sent, LANES), dtype),
                pltpu.VMEM((chips, rows, LANES), BF16),
                pltpu.VMEM((chips, rows, LANES), BF16),
            ]

        total_scratch = [
            pltpu.VMEM((peers, tokens // peers, LANES), F32),
            pltpu.VMEM((peers, tokens // peers, LANES), F32),
            pltpu.VMEM((tokens // peers, LANES), F32),
            pltpu.VMEM((peers, tokens // peers, LANES), F32),
        ]
        half = chips // 2
        return pl.pallas_call(
            functools.partial(kernel, chips, peers),
            out_shape=(
                pltpu.VMEM(w_in.shape, F32),
                pltpu.VMEM(b_in.shape, F32),
                pltpu.VMEM(c_in.shape, F32),
            ),
            in_specs=[hbm] * 5 + [pl.BlockSpec(memory_space=pltpu.SMEM), hbm],
            out_specs=(vmem, vmem, vmem),
            scratch_shapes=[
                pltpu.VMEM(inputs.shape, BF16),
                pltpu.VMEM(b_in.shape, BF16),
                pltpu.VMEM(c_in.shape, BF16),
                pltpu.VMEM(log_decay.shape[::-1], F32),
                pltpu.VMEM(d_out.shape, BF16),
                pltpu.VMEM((devices, tokens, width), BF16),
                pltpu.VMEM((devices, tokens, width), BF16),
                pltpu.VMEM((chips, 2 * tokens // peers, 2 * LANES), BF16),
                pltpu.VMEM((chips, peers, 2 * tokens // peers, LANES), BF16),
            ]
            + carry_scratch(rows + 8, F32)
            + carry_scratch(rows, BF16)
            + total_scratch * 2
            + [
                pltpu.SemaphoreType.DMA((4,)),
                pltpu.SemaphoreType.DMA((2, half + 1, 2 * max(RING_W[1], RING_G[1]))),
                pltpu.SemaphoreType.DMA((2, half + 1)),
                pltpu.SemaphoreType.DMA((2, 8)),
                pltpu.SemaphoreType.DMA((2, 4)),
                pltpu.SemaphoreType.DMA((6,)),
                pltpu.SemaphoreType.DMA((6,)),
                pltpu.SemaphoreType.REGULAR((3,)),
            ],
            compiler_params=pltpu.CompilerParams(
                collective_id=0, has_side_effects=True, vmem_limit_bytes=60 * 1024 * 1024
            ),
        )(inputs, w_in, b_in, c_in, log_decay.T, skip, d_out)

    return jax.shard_map(
        per_device,
        mesh=mesh,
        in_specs=(
            P("ctx", None),
            P("ctx", "tp"),
            P("ctx", None),
            P("ctx", None),
            P("ctx", "tp"),
            P("tp"),
            P("ctx", "tp"),
        ),
        out_specs=(P("ctx", "tp"), P("ctx", None), P("ctx", None)),
        check_vma=False,
    )
```
